32 devices in a mesh: dp: 4 (over y, core), mp: 8 (over z, x).
Axes of the slice: x: 2, y: 2, z: 4, core: 2. Of those that a mesh axis runs over, the one named last changes fastest.
Arguments:
- tokens: bfloat16 [128, 3072], P(('dp', 'mp')), may hold values from -6 to 6
- cotangent: bfloat16 [128, 3072], P(('dp', 'mp')), may hold values from -6 to 6
- up_weight: bfloat16 [3072, 12288], P(None, 'mp'), may hold values from -0.109375 to 0.109375
- down_weight: bfloat16 [12288, 3072], P('mp'), may hold values from -0.0546875 to 0.0546875
Outputs:
- mixed_out: bfloat16 [128, 3072], P(('dp', 'mp'))
- token_gradient: bfloat16 [128, 3072], P(('dp', 'mp'))
- up_grad: bfloat16 [3072, 12288], P('dp', 'mp')
- down_grad: bfloat16 [12288, 3072], P('mp', 'dp')
The draws below stay inside these ranges and needn't reach their ends.
All inputs are finite; a program needn't handle non-finite values.
Results may differ from the reference program's by a relative error of at most 0.02.
Values may be sent and summed in bfloat16 or wider, within the bound.
A program may use at most 128 MiB of HBM per device.

```python
import jax
import jax.numpy as jnp
from jax import lax

D = 3072
FF = 12288
SHARD_TOK = 32
TOKENS = 128
N_DP = 4
N_MP = 8


def spiked(result, key, source, target, shards_of, factor):
    def block_of(dim):
        return (jnp.arange(result.shape[dim]) // (result.shape[dim] // shards_of)).reshape((-1,) + (1,) * (result.ndim - 1 - dim))

    near = jax.random.permutation(key, shards_of)[block_of(target)]
    far = (block_of(target) + shards_of // 2) % shards_of
    return jnp.where((block_of(source) == near) | (block_of(source) == far), factor * result, result)


def block_levels(rng, dims, split, smallest, high):
    def one(position, shards_of):
        steps = jax.random.uniform(jax.random.fold_in(jax.random.fold_in(rng, 6), position), (shards_of,), jnp.float32, smallest / len(split), high / len(split))
        return jnp.repeat(jnp.exp(steps), dims[position] // shards_of).reshape((-1,) + (1,) * (len(dims) - position - 1))

    loudness = one(*split[0])
    for cut in split[1:]:
        loudness = loudness * one(*cut)
    return loudness


def scatter_about(rng, dims, scale, most, split=(), held_as=jnp.bfloat16):
    entries = scale * jax.random.normal(rng, dims, jnp.float32)
    if split:
        entries = entries * block_levels(rng, dims, split, -0.22, 0.18)
    return jnp.clip(entries, -most, most).astype(held_as)


def gaussian_with(own_key, extent, spread, bound, split, heavy, kind=jnp.bfloat16):
    result = spread * jax.random.normal(own_key, extent, jnp.float32)
    if split:
        result = result * block_levels(own_key, extent, split, -0.22, 0.18)
    return jnp.clip(spiked(result, jax.random.fold_in(own_key, 3), *heavy), -bound, bound).astype(kind)


def setup_inputs(seed: int = 0) -> dict:
    key_list = jax.random.split(jax.random.key(seed), 5)
    return {
        "tokens": gaussian_with(key_list[0], (TOKENS, D), 1.0, 6.0, ((0, 32),), (0, 1, 32, 2.75)),
        "cotangent": gaussian_with(key_list[1], (TOKENS, D), 1.0, 6.0, ((0, 32),), (0, 1, 32, 2.75)),
        "up_weight": scatter_about(key_list[2], (D, FF), D ** -0.5, 0.109375, ((1, 8),)),
        "down_weight": scatter_about(key_list[3], (FF, D), FF ** -0.5, 0.0546875, ((0, 8),)),
    }


root_half = 0.7071067811865476
density_scale = 0.3989422804014327

def standardise_rows(tokens):
    values = tokens.astype(jnp.float32)
    row_mean = lax.optimization_barrier(jnp.mean(values, axis=1, keepdims=True))
    centred = values - row_mean
    variance = lax.optimization_barrier(jnp.mean(centred * centred, axis=1, keepdims=True))
    reciprocal_spread = lax.rsqrt(variance + 1e-06)
    return (centred * reciprocal_spread, reciprocal_spread)

def gelu_parts(pre_act):
    cumulative = 0.5 * (1.0 + lax.erf(pre_act * root_half))
    density = jnp.exp(-0.5 * pre_act * pre_act) * density_scale
    return (pre_act * cumulative, cumulative + pre_act * density)

def rounded(values):
    return lax.optimization_barrier(values.astype(jnp.bfloat16)).astype(jnp.float32)

def reference(tokens, cotangent, up_weight, down_weight):
    centred_scaled_input, reciprocal_spread = standardise_rows(tokens)
    standardised_input = centred_scaled_input.astype(jnp.bfloat16)
    pre_act = jnp.dot(standardised_input, up_weight, preferred_element_type=jnp.float32)
    gelu_value, gelu_slope = gelu_parts(pre_act)
    hidden = gelu_value.astype(jnp.bfloat16)
    block_width = FF // N_MP

    def out_step(running, block):
        first_unit = (block * block_width).astype(jnp.int32)
        hid_block = lax.dynamic_slice_in_dim(hidden, first_unit, block_width, 1)
        down_block = lax.dynamic_slice_in_dim(down_weight, first_unit, block_width, 0)
        return (running + rounded(jnp.dot(hid_block, down_block, preferred_element_type=jnp.float32)), None)
    start_rows = jnp.zeros((TOKENS, D), jnp.float32)
    block_ids = jnp.arange(N_MP, dtype=jnp.int32)
    block_out, _ = lax.scan(out_step, start_rows, block_ids)
    mixed_out = (tokens.astype(jnp.float32) + block_out).astype(jnp.bfloat16)
    hidden_grad = jnp.dot(cotangent, down_weight.T, preferred_element_type=jnp.float32)
    act_grad = (hidden_grad * gelu_slope).astype(jnp.bfloat16)

    def back_step(running, block):
        first_unit = (block * block_width).astype(jnp.int32)
        grad_block = lax.dynamic_slice_in_dim(act_grad, first_unit, block_width, 1)
        up_block = lax.dynamic_slice_in_dim(up_weight, first_unit, block_width, 1)
        return (running + rounded(jnp.dot(grad_block, up_block.T, preferred_element_type=jnp.float32)), None)
    standardised_gradient, _ = lax.scan(back_step, start_rows, block_ids)
    gradient_average = lax.optimization_barrier(jnp.mean(standardised_gradient, axis=1, keepdims=True))
    projection_average = lax.optimization_barrier(jnp.mean(standardised_gradient * centred_scaled_input, axis=1, keepdims=True))
    token_gradient = cotangent.astype(jnp.float32) + reciprocal_spread * (standardised_gradient - gradient_average - centred_scaled_input * projection_average)
    token_gradient = token_gradient.astype(jnp.bfloat16)

    def shard_step(carry, shard):
        up_sum, down_sum = carry
        first_row = (shard * SHARD_TOK).astype(jnp.int32)
        hid_rows = lax.dynamic_slice_in_dim(hidden, first_row, SHARD_TOK, 0)
        cot_rows = lax.dynamic_slice_in_dim(cotangent, first_row, SHARD_TOK, 0)
        norm_rows = lax.dynamic_slice_in_dim(standardised_input, first_row, SHARD_TOK, 0)
        act_rows = lax.dynamic_slice_in_dim(act_grad, first_row, SHARD_TOK, 0)
        down_sum = down_sum + rounded(jnp.dot(hid_rows.T, cot_rows, preferred_element_type=jnp.float32))
        up_sum = up_sum + rounded(jnp.dot(norm_rows.T, act_rows, preferred_element_type=jnp.float32))
        return ((up_sum, down_sum), None)
    start_grads = (jnp.zeros((D, FF), jnp.float32), jnp.zeros((FF, D), jnp.float32))
    (up_sum, down_sum), _ = lax.scan(shard_step, start_grads, jnp.arange(N_DP, dtype=jnp.int32))
    return (mixed_out, token_gradient, up_sum.astype(jnp.bfloat16), down_sum.astype(jnp.bfloat16))
```

```python
import functools

import jax
import jax.numpy as jnp
from jax import lax
from jax.experimental import pallas as pl
from jax.experimental.pallas import tpu as pltpu
from jax.sharding import PartitionSpec as P

ROOT_HALF = 0.7071067811865476
DENSITY_SCALE = 0.3989422804014327
TILE_ROWS = 16
MESH = pl.DeviceIdType.MESH
F32 = jnp.float32
BF16 = jnp.bfloat16


def chunk_of(size, choices=(512, 384, 256)):
    for choice in choices:
        if size % choice == 0:
            return choice
    return size


def dot(left, right, left_dim=1, right_dim=0):
    return lax.dot_general(
        left, right, (((left_dim,), (right_dim,)), ((), ())), preferred_element_type=F32
    )


def one_hot(shape, wanted):
    return jnp.where(wanted, 1.0, 0.0).astype(BF16)


def kernel(
    n_dp, n_mp,
    tokens_ref, cot_ref, up_hbm, down_hbm,
    mixed_ref, tgrad_ref, up_grad_hbm, down_grad_hbm,
    up_v, down_v,
    gather_n, gather_c,
    rs_out_send, rs_out, rs_grad_send, rs_grad,
    ncol_send, ccol_send, ncol, ccol,
    hid, act, slope, rows_n, rows_c,
    up_out, down_out,
    load_sem, out_sem, mp_send, mp_recv, dp_send, dp_recv,
):
    rows, width = tokens_ref.shape
    pieces = TILE_ROWS // rows
    wide = width // pieces
    shard_rows = rows * n_mp
    packed_rows = TILE_ROWS * n_mp
    units = up_v.shape[1]
    feats = width // n_dp
    dp = lax.axis_index("dp")
    mp = lax.axis_index("mp")

    def dp_peer(o):
        return {"dp": lax.rem(dp + o, n_dp), "mp": mp}

    def mp_peer(o):
        return {"dp": dp, "mp": lax.rem(mp + o, n_mp)}

    loads = []
    parts = load_sem.shape[1]
    for w, (src, dst) in enumerate(((up_hbm, up_v), (down_hbm, down_v))):
        step = src.shape[0] // parts
        for i in range(parts):
            where = pl.ds(i * step, step)
            copy = pltpu.make_async_copy(src.at[where], dst.at[where], load_sem.at[w, i])
            copy.start()
            loads.append(copy)

    barrier = pltpu.get_barrier_semaphore()
    for o in range(1, n_mp):
        pl.semaphore_signal(barrier, inc=1, device_id=mp_peer(o), device_id_type=MESH)
    for o in range(1, n_dp):
        pl.semaphore_signal(barrier, inc=1, device_id=dp_peer(o), device_id_type=MESH)

    sent = []

    def send_mp(kind, src, dst, o):
        copy = pltpu.make_async_remote_copy(
            src_ref=src, dst_ref=dst,
            send_sem=mp_send.at[kind, o], recv_sem=mp_recv.at[kind, o],
            device_id=mp_peer(o), device_id_type=MESH,
        )
        copy.start()
        sent.append(copy)
        return copy

    def send_dp(kind, src, dst, o):
        copy = pltpu.make_async_remote_copy(
            src_ref=src, dst_ref=dst,
            send_sem=dp_send.at[kind, o], recv_sem=dp_recv.at[kind, o],
            device_id=dp_peer(o), device_id_type=MESH,
        )
        copy.start()
        sent.append(copy)
        return copy

    tokens = tokens_ref[...].astype(F32)
    centred = tokens - jnp.mean(tokens, axis=1, keepdims=True)
    variance = jnp.mean(centred * centred, axis=1, keepdims=True)
    inverse = lax.rsqrt(variance + 1e-06)
    xhat = centred * inverse
    cot = cot_ref[...].astype(F32)

    def pack(values):
        return jnp.concatenate(
            [values[:, q * wide:(q + 1) * wide] for q in range(pieces)], axis=0
        ).astype(BF16)

    gather_n[0] = pack(xhat)
    gather_c[0] = pack(cot)

    pl.semaphore_wait(barrier, n_mp - 1 + n_dp - 1)
    got_n = [send_mp(0, gather_n.at[0], gather_n.at[o], o) for o in range(1, n_mp)]
    got_c = [send_mp(1, gather_c.at[0], gather_c.at[o], o) for o in range(1, n_mp)]

    at = lax.broadcasted_iota(jnp.int32, (shard_rows, packed_rows), 0)
    to = lax.broadcasted_iota(jnp.int32, (shard_rows, packed_rows), 1)
    home = at + (at // rows) * (TILE_ROWS - rows)
    unpackers = [one_hot(None, to == home + q * rows) for q in range(pieces)]
    at = lax.broadcasted_iota(jnp.int32, (8, packed_rows), 0)
    to = lax.broadcasted_iota(jnp.int32, (8, packed_rows), 1) % TILE_ROWS
    adders = [one_hot(None, (to == at + q * rows) & (at < rows)) for q in range(pieces)]

    def unpack(gathered, out):
        flat = gathered[...].reshape(packed_rows, wide)
        for q in range(pieces):
            out[:, q * wide:(q + 1) * wide] = dot(unpackers[q], flat).astype(BF16)

    def send_columns(kind, out, blocks, slots):
        for j in range(n_dp):
            blocks[j] = out[:, j * feats:(j + 1) * feats]
        got = [
            send_dp(kind, blocks.at[lax.rem(dp + o, n_dp)], slots.at[o], o)
            for o in range(1, n_dp)
        ]
        slots[0] = blocks[dp]
        return got

    for copy in got_n:
        copy.wait_recv()
    unpack(gather_n, rows_n)
    got_ncol = send_columns(0, rows_n, ncol_send, ncol)

    for copy in loads[:parts]:
        copy.wait()
    step = chunk_of(units)
    for i in range(units // step):
        cols = slice(i * step, (i + 1) * step)
        pre_act = dot(rows_n[...], up_v[:, cols])
        cumulative = 0.5 * (1.0 + lax.erf(pre_act * ROOT_HALF))
        density = jnp.exp(-0.5 * pre_act * pre_act) * DENSITY_SCALE
        hid[0, :, cols] = (pre_act * cumulative).astype(BF16)
        slope[:, cols] = cumulative + pre_act * density
    got_hid = [send_dp(2, hid.at[0], hid.at[o], o) for o in range(1, n_dp)]

    for copy in got_c:
        copy.wait_recv()
    unpack(gather_c, rows_c)
    got_ccol = send_columns(1, rows_c, ccol_send, ccol)

    for copy in loads[parts:]:
        copy.wait()

    def scatter(kind, partial_of, send, slots):
        total = jnp.zeros((packed_rows, wide), F32)
        for q in range(pieces):
            total += dot(unpackers[q], partial_of(q).astype(BF16), 0, 0)
        send[...] = total.astype(BF16).reshape(n_mp, TILE_ROWS, wide)
        got = [
            send_mp(kind, send.at[n_mp - o], slots.at[o], o) for o in range(1, n_mp)
        ]
        slots[0] = send[0]
        return got

    got_out = scatter(
        2, lambda q: dot(hid[0], down_v[:, q * wide:(q + 1) * wide]), rs_out_send, rs_out
    )

    for i in range(units // step):
        cols = slice(i * step, (i + 1) * step)
        hidden_grad = dot(rows_c[...], down_v[cols, :], 1, 1)
        act[0, :, cols] = (hidden_grad * slope[:, cols]).astype(BF16)
    got_act = [send_dp(3, act.at[0], act.at[o], o) for o in range(1, n_dp)]

    got_grad = scatter(
        3, lambda q: dot(act[0], up_v[q * wide:(q + 1) * wide, :], 1, 1), rs_grad_send, rs_grad
    )

    stores = []

    def weight_grad(left, right, out, out_hbm, which):
        lefts = left.shape[2]
        step = chunk_of(lefts)
        right_rows = right[...].reshape(n_dp * shard_rows, right.shape[2])
        for i in range(lefts // step):
            cols = slice(i * step, (i + 1) * step)
            left_rows = left[:, :, cols].reshape(n_dp * shard_rows, step)
            out[cols, :] = dot(left_rows, right_rows, 0, 0).astype(BF16)
            copy = pltpu.make_async_copy(out.at[cols], out_hbm.at[cols], out_sem.at[which, i])
            copy.start()
            stores.append(copy)

    for copy in got_ccol + got_hid:
        copy.wait_recv()
    weight_grad(hid, ccol, down_out, down_grad_hbm, 0)
    for copy in got_ncol + got_act:
        copy.wait_recv()
    weight_grad(ncol, act, up_out, up_grad_hbm, 1)

    def summed(got, slots):
        for copy in got:
            copy.wait_recv()
        flat = slots[...].reshape(packed_rows, wide)
        return jnp.concatenate([dot(adders[q], flat)[:rows] for q in range(pieces)], axis=1)

    block_out = summed(got_out, rs_out)
    mixed_ref[...] = (tokens + block_out).astype(BF16)
    grad = summed(got_grad, rs_grad)
    grad_mean = jnp.mean(grad, axis=1, keepdims=True)
    projection = jnp.mean(grad * xhat, axis=1, keepdims=True)
    tgrad_ref[...] = (cot + inverse * (grad - grad_mean - xhat * projection)).astype(BF16)

    for copy in stores:
        copy.wait()
    for copy in sent:
        copy.wait_send()


def body(n_dp, n_mp, tokens, cotangent, up_weight, down_weight):
    rows, width = tokens.shape
    units = up_weight.shape[1]
    feats = width // n_dp
    shard_rows = rows * n_mp
    wide = width * rows // TILE_ROWS
    packed = pltpu.VMEM((n_mp, TILE_ROWS, wide), BF16)
    columns = pltpu.VMEM((n_dp, shard_rows, feats), BF16)
    hiddens = pltpu.VMEM((n_dp, shard_rows, units), BF16)
    macs = 4 * shard_rows * width * units + 2 * n_dp * shard_rows * units * feats
    return pl.pallas_call(
        functools.partial(kernel, n_dp, n_mp),
        out_shape=(
            jax.ShapeDtypeStruct(tokens.shape, BF16),
            jax.ShapeDtypeStruct(tokens.shape, BF16),
            jax.ShapeDtypeStruct((feats, units), BF16),
            jax.ShapeDtypeStruct((units, feats), BF16),
        ),
        in_specs=[pl.BlockSpec(memory_space=pltpu.VMEM)] * 2
        + [pl.BlockSpec(memory_space=pl.ANY)] * 2,
        out_specs=[pl.BlockSpec(memory_space=pltpu.VMEM)] * 2
        + [pl.BlockSpec(memory_space=pl.ANY)] * 2,
        scratch_shapes=[
            pltpu.VMEM(up_weight.shape, BF16),
            pltpu.VMEM(down_weight.shape, BF16),
            packed, packed,
            packed, packed, packed, packed,
            columns, columns, columns, columns,
            hiddens, hiddens,
            pltpu.VMEM((shard_rows, units), F32),
            pltpu.VMEM((shard_rows, width), BF16),
            pltpu.VMEM((shard_rows, width), BF16),
            pltpu.VMEM((feats, units), BF16),
            pltpu.VMEM((units, feats), BF16),
            pltpu.SemaphoreType.DMA((2, 4)),
            pltpu.SemaphoreType.DMA((2, 8)),
            pltpu.SemaphoreType.DMA((4, n_mp)),
            pltpu.SemaphoreType.DMA((4, n_mp)),
            pltpu.SemaphoreType.DMA((4, n_dp)),
            pltpu.SemaphoreType.DMA((4, n_dp)),
        ],
        compiler_params=pltpu.CompilerParams(
            collective_id=0, has_side_effects=True, vmem_limit_bytes=56 * 1024 * 1024
        ),
        cost_estimate=pl.CostEstimate(
            flops=2 * macs, bytes_accessed=4 * width * units, transcendentals=2 * shard_rows * units
        ),
    )(tokens, cotangent, up_weight, down_weight)


def solution(mesh):
    return jax.shard_map(
        functools.partial(body, mesh.shape["dp"], mesh.shape["mp"]),
        mesh=mesh,
        in_specs=(P(("dp", "mp"), None), P(("dp", "mp"), None), P(None, "mp"), P("mp", None)),
        out_specs=(P(("dp", "mp"), None), P(("dp", "mp"), None), P("dp", "mp"), P("mp", "dp")),
        check_vma=False,
    )
```

```python
import functools

import jax
import jax.numpy as jnp
from jax import lax
from jax.experimental import pallas as pl
from jax.experimental.pallas import tpu as pltpu
from jax.sharding import PartitionSpec as P

ROOT_HALF = 0.7071067811865476
DENSITY_SCALE = 0.3989422804014327
TILE_ROWS = 16
MESH = pl.DeviceIdType.MESH
F32 = jnp.float32
BF16 = jnp.bfloat16


def chunk_of(size, choices=(512, 384, 256)):
    for choice in choices:
        if size % choice == 0:
            return choice
    return size


def dot(left, right, left_dim=1, right_dim=0):
    return lax.dot_general(
        left, right, (((left_dim,), (right_dim,)), ((), ())), preferred_element_type=F32
    )


def one_hot(wanted):
    return jnp.where(wanted, 1.0, 0.0).astype(BF16)


def relay_group(axis, n, send_sem, recv_sem, sent):
    other_axis = "mp" if axis == "dp" else "dp"
    me, fixed = lax.axis_index(axis), lax.axis_index(other_axis)
    lines = n // 2
    line, side = me // 2, me % 2

    def peer(block):
        to_line = lax.rem(line + block // 2, lines)
        to_side = side if block % 2 == 0 else 1 - side
        return {axis: 2 * to_line + to_side, other_axis: fixed}

    def start(kind, src, dst, block, to=None):
        copy = pltpu.make_async_remote_copy(
            src_ref=src, dst_ref=dst,
            send_sem=send_sem.at[kind, block], recv_sem=recv_sem.at[kind, block],
            device_id=peer(block if to is None else to), device_id_type=MESH,
        )
        copy.start()
        sent.append(copy)
        return copy

    def spread(kind, src, slots):
        straight = [start(kind, src, slots.at[2 * k], 2 * k) for k in range(1, lines)]
        return straight, [start(kind, src, slots.at[1], 1)]

    def pass_on(kind, slots, straight, crossed):
        for k in range(1, lines):
            straight[k - 1].wait_recv()
            crossed.append(start(kind, slots.at[2 * k], slots.at[2 * k + 1], 2 * k + 1, to=1))

    def opposite(block):
        return 2 * ((lines - block // 2) % lines) + block % 2

    return peer, start, spread, pass_on, opposite


def row_norm(tokens):
    centred = tokens - jnp.mean(tokens, axis=1, keepdims=True)
    variance = jnp.mean(centred * centred, axis=1, keepdims=True)
    inverse = lax.rsqrt(variance + 1e-06)
    return centred * inverse, inverse


def exchange_kernel(
    n_dp, n_mp,
    tokens_ref, cot_ref, up_hbm, down_hbm,
    rs_out, rs_grad, ncol, ccol, hid, act,
    up_v, down_v,
    gather_n, gather_c, rs_out_send, rs_grad_send,
    ncol_send, ccol_send, hid_own, act_own, slope, rows_n, rows_c,
    load_sem, own_sem, mp_send, mp_recv, dp_send, dp_recv,
):
    rows, width = tokens_ref.shape
    pieces = TILE_ROWS // rows
    wide = width // pieces
    shard_rows = rows * n_mp
    packed_rows = TILE_ROWS * n_mp
    units = up_v.shape[1]
    feats = width // n_dp

    loads = []
    parts = load_sem.shape[1]
    for w, (src, dst) in enumerate(((up_hbm, up_v), (down_hbm, down_v))):
        step = src.shape[0] // parts
        for i in range(parts):
            where = pl.ds(i * step, step)
            copy = pltpu.make_async_copy(src.at[where], dst.at[where], load_sem.at[w, i])
            copy.start()
            loads.append(copy)

    sent = []
    mp_peer, mp_start, mp_spread, mp_pass_on, mp_opposite = relay_group(
        "mp", n_mp, mp_send, mp_recv, sent
    )
    dp_peer, dp_start, dp_spread, dp_pass_on, dp_opposite = relay_group(
        "dp", n_dp, dp_send, dp_recv, sent
    )
    barrier = pltpu.get_barrier_semaphore()
    for b in range(1, n_mp):
        pl.semaphore_signal(barrier, inc=1, device_id=mp_peer(b), device_id_type=MESH)
    for b in range(1, n_dp):
        pl.semaphore_signal(barrier, inc=1, device_id=dp_peer(b), device_id_type=MESH)

    def pack(values):
        return jnp.concatenate(
            [values[:, q * wide:(q + 1) * wide] for q in range(pieces)], axis=0
        ).astype(BF16)

    xhat, _ = row_norm(tokens_ref[...].astype(F32))
    gather_n[0] = pack(xhat)
    gather_c[0] = pack(cot_ref[...].astype(F32))

    pl.semaphore_wait(barrier, n_mp - 1 + n_dp - 1)
    straight_n, crossed_n = mp_spread(0, gather_n.at[0], gather_n)
    straight_c, crossed_c = mp_spread(1, gather_c.at[0], gather_c)

    at = lax.broadcasted_iota(jnp.int32, (shard_rows, packed_rows), 0)
    to = lax.broadcasted_iota(jnp.int32, (shard_rows, packed_rows), 1)
    home = at + (at // rows) * (TILE_ROWS - rows)
    unpackers = [one_hot(to == home + q * rows) for q in range(pieces)]

    def unpack(gathered, out):
        flat = gathered[...].reshape(packed_rows, wide)
        for q in range(pieces):
            out[:, q * wide:(q + 1) * wide] = dot(unpackers[q], flat).astype(BF16)

    own = []

    def keep(src, slots, which):
        copy = pltpu.make_async_copy(src, slots.at[0], own_sem.at[which])
        copy.start()
        own.append(copy)

    def send_columns(kind, out, blocks, slots):
        for j in range(n_dp):
            blocks[j] = out[:, j * feats:(j + 1) * feats]
        got = [
            dp_start(kind, blocks.at[dp_peer(b)["dp"]], slots.at[b], b) for b in range(1, n_dp)
        ]
        keep(blocks.at[lax.axis_index("dp")], slots, kind)
        return got

    mp_pass_on(0, gather_n, straight_n, crossed_n)
    mp_pass_on(1, gather_c, straight_c, crossed_c)
    for copy in crossed_n:
        copy.wait_recv()
    unpack(gather_n, rows_n)
    arrivals = send_columns(0, rows_n, ncol_send, ncol)

    for copy in loads[:parts]:
        copy.wait()
    step = chunk_of(units)
    for i in range(units // step):
        cols = slice(i * step, (i + 1) * step)
        pre_act = dot(rows_n[...], up_v[:, cols])
        cumulative = 0.5 * (1.0 + lax.erf(pre_act * ROOT_HALF))
        density = jnp.exp(-0.5 * pre_act * pre_act) * DENSITY_SCALE
        hid_own[:, cols] = (pre_act * cumulative).astype(BF16)
        slope[:, cols] = cumulative + pre_act * density
    straight_h, crossed_h = dp_spread(2, hid_own, hid)
    keep(hid_own, hid, 2)

    for copy in crossed_c:
        copy.wait_recv()
    unpack(gather_c, rows_c)
    arrivals += send_columns(1, rows_c, ccol_send, ccol)

    for copy in loads[parts:]:
        copy.wait()

    def scatter(kind, partial_of, send, slots):
        total = jnp.zeros((packed_rows, wide), F32)
        for q in range(pieces):
            total += dot(unpackers[q], partial_of(q).astype(BF16), 0, 0)
        send[...] = total.astype(BF16).reshape(n_mp, TILE_ROWS, wide)
        got = [mp_start(kind, send.at[mp_opposite(b)], slots.at[b], b) for b in range(1, n_mp)]
        keep(send.at[0], slots, 2 + kind)
        return got

    arrivals += scatter(
        2, lambda q: dot(hid_own[...], down_v[:, q * wide:(q + 1) * wide]), rs_out_send, rs_out
    )
    for i in range(units // step):
        cols = slice(i * step, (i + 1) * step)
        hidden_grad = dot(rows_c[...], down_v[cols, :], 1, 1)
        act_own[:, cols] = (hidden_grad * slope[:, cols]).astype(BF16)
    straight_a, crossed_a = dp_spread(3, act_own, act)
    keep(act_own, act, 3)
    dp_pass_on(2, hid, straight_h, crossed_h)
    arrivals += scatter(
        3, lambda q: dot(act_own[...], up_v[q * wide:(q + 1) * wide, :], 1, 1), rs_grad_send, rs_grad
    )
    dp_pass_on(3, act, straight_a, crossed_a)

    for copy in arrivals + crossed_h + crossed_a:
        copy.wait_recv()
    for copy in own:
        copy.wait()
    for copy in sent:
        copy.wait_send()


def result_kernel(
    tokens_ref, cot_ref, rs_out, rs_grad, ncol, ccol, hid, act,
    mixed_ref, tgrad_ref, up_grad_hbm, down_grad_hbm,
    up_out, down_out, out_sem,
):
    rows, width = tokens_ref.shape
    pieces = TILE_ROWS // rows
    n_mp, _, wide = rs_out.shape
    packed_rows = TILE_ROWS * n_mp
    stores = []

    def weight_grad(left, right, out, out_hbm, which):
        n_dp, shard_rows, lefts = left.shape
        step = chunk_of(lefts)
        right_rows = right[...].reshape(n_dp * shard_rows, right.shape[2])
        for i in range(lefts // step):
            cols = slice(i * step, (i + 1) * step)
            left_rows = left[:, :, cols].reshape(n_dp * shard_rows, step)
            out[cols, :] = dot(left_rows, right_rows, 0, 0).astype(BF16)
            copy = pltpu.make_async_copy(out.at[cols], out_hbm.at[cols], out_sem.at[which, i])
            copy.start()
            stores.append(copy)

    weight_grad(hid, ccol, down_out, down_grad_hbm, 0)
    weight_grad(ncol, act, up_out, up_grad_hbm, 1)

    at = lax.broadcasted_iota(jnp.int32, (8, packed_rows), 0)
    to = lax.broadcasted_iota(jnp.int32, (8, packed_rows), 1) % TILE_ROWS
    adders = [one_hot((to == at + q * rows) & (at < rows)) for q in range(pieces)]

    def summed(slots):
        flat = slots[...].reshape(packed_rows, wide)
        return jnp.concatenate([dot(adders[q], flat)[:rows] for q in range(pieces)], axis=1)

    tokens = tokens_ref[...].astype(F32)
    xhat, inverse = row_norm(tokens)
    mixed_ref[...] = (tokens + summed(rs_out)).astype(BF16)
    grad = summed(rs_grad)
    grad_mean = jnp.mean(grad, axis=1, keepdims=True)
    projection = jnp.mean(grad * xhat, axis=1, keepdims=True)
    tgrad_ref[...] = (
        cot_ref[...].astype(F32) + inverse * (grad - grad_mean - xhat * projection)
    ).astype(BF16)
    for copy in stores:
        copy.wait()


def body(n_dp, n_mp, tokens, cotangent, up_weight, down_weight):
    rows, width = tokens.shape
    units = up_weight.shape[1]
    feats = width // n_dp
    shard_rows = rows * n_mp
    wide = width * rows // TILE_ROWS
    packed = (n_mp, TILE_ROWS, wide)
    columns = (n_dp, shard_rows, feats)
    hiddens = (n_dp, shard_rows, units)
    in_vmem, anywhere = pl.BlockSpec(memory_space=pltpu.VMEM), pl.BlockSpec(memory_space=pl.ANY)
    exchanged = pl.pallas_call(
        functools.partial(exchange_kernel, n_dp, n_mp),
        out_shape=[
            jax.ShapeDtypeStruct(shape, BF16)
            for shape in (packed, packed, columns, columns, hiddens, hiddens)
        ],
        in_specs=[in_vmem] * 2 + [anywhere] * 2,
        out_specs=[anywhere] * 6,
        scratch_shapes=[
            pltpu.VMEM(up_weight.shape, BF16),
            pltpu.VMEM(down_weight.shape, BF16),
            *[pltpu.VMEM(packed, BF16)] * 4,
            *[pltpu.VMEM(columns, BF16)] * 2,
            *[pltpu.VMEM(hiddens[1:], BF16)] * 2,
            pltpu.VMEM((shard_rows, units), F32),
            *[pltpu.VMEM((shard_rows, width), BF16)] * 2,
            pltpu.SemaphoreType.DMA((2, 4)),
            pltpu.SemaphoreType.DMA((6,)),
            pltpu.SemaphoreType.DMA((4, n_mp)),
            pltpu.SemaphoreType.DMA((4, n_mp)),
            pltpu.SemaphoreType.DMA((4, n_dp)),
            pltpu.SemaphoreType.DMA((4, n_dp)),
        ],
        compiler_params=pltpu.CompilerParams(
            collective_id=0, has_side_effects=True, vmem_limit_bytes=56 * 1024 * 1024
        ),
        cost_estimate=pl.CostEstimate(
            flops=8 * shard_rows * width * units,
            bytes_accessed=4 * width * units,
            transcendentals=2 * shard_rows * units,
        ),
    )(tokens, cotangent, up_weight, down_weight)
    return pl.pallas_call(
        result_kernel,
        out_shape=(
            jax.ShapeDtypeStruct(tokens.shape, BF16),
            jax.ShapeDtypeStruct(tokens.shape, BF16),
            jax.ShapeDtypeStruct((feats, units), BF16),
            jax.ShapeDtypeStruct((units, feats), BF16),
        ),
        in_specs=[in_vmem] * 8,
        out_specs=[in_vmem] * 2 + [anywhere] * 2,
        scratch_shapes=[
            pltpu.VMEM((feats, units), BF16),
            pltpu.VMEM((units, feats), BF16),
            pltpu.SemaphoreType.DMA((2, 8)),
        ],
        compiler_params=pltpu.CompilerParams(vmem_limit_bytes=24 * 1024 * 1024),
        cost_estimate=pl.CostEstimate(
            flops=4 * n_dp * shard_rows * units * feats,
            bytes_accessed=4 * feats * units,
            transcendentals=0,
        ),
    )(tokens, cotangent, *exchanged)


def solution(mesh):
    return jax.shard_map(
        functools.partial(body, mesh.shape["dp"], mesh.shape["mp"]),
        mesh=mesh,
        in_specs=(P(("dp", "mp"), None), P(("dp", "mp"), None), P(None, "mp"), P("mp", None)),
        out_specs=(P(("dp", "mp"), None), P(("dp", "mp"), None), P("dp", "mp"), P("mp", "dp")),
        check_vma=False,
    )
```

```python
import functools

import jax
import jax.numpy as jnp
from jax import lax
from jax.experimental import pallas as pl
from jax.experimental.pallas import tpu as pltpu
from jax.sharding import PartitionSpec as P

ROOT_HALF = 0.7071067811865476
DENSITY_SCALE = 0.3989422804014327
TILE_ROWS = 16
MESH = pl.DeviceIdType.MESH
F32 = jnp.float32
BF16 = jnp.bfloat16


def chunk_of(size, choices=(512, 384, 256)):
    for choice in choices:
        if size % choice == 0:
            return choice
    return size


def dot(left, right, left_dim=1, right_dim=0):
    return lax.dot_general(
        left, right, (((left_dim,), (right_dim,)), ((), ())), preferred_element_type=F32
    )


def one_hot(wanted):
    return jnp.where(wanted, 1.0, 0.0).astype(BF16)


def relay_group(axis, n, send_sem, recv_sem, sent):
    other_axis = "mp" if axis == "dp" else "dp"
    me, fixed = lax.axis_index(axis), lax.axis_index(other_axis)
    lines = n // 2
    line, side = me // 2, me % 2

    def peer(block):
        to_line = lax.rem(line + block // 2, lines)
        to_side = side if block % 2 == 0 else 1 - side
        return {axis: 2 * to_line + to_side, other_axis: fixed}

    def start(kind, src, dst, block, to=None):
        copy = pltpu.make_async_remote_copy(
            src_ref=src, dst_ref=dst,
            send_sem=send_sem.at[kind, block], recv_sem=recv_sem.at[kind, block],
            device_id=peer(block if to is None else to), device_id_type=MESH,
        )
        copy.start()
        sent.append(copy)
        return copy

    def spread(kind, src, slots):
        straight = [start(kind, src, slots.at[2 * k], 2 * k) for k in range(1, lines)]
        return straight, [start(kind, src, slots.at[1], 1)]

    def pass_on(kind, slots, straight, crossed):
        for k in range(1, lines):
            straight[k - 1].wait_recv()
            crossed.append(start(kind, slots.at[2 * k], slots.at[2 * k + 1], 2 * k + 1, to=1))

    def opposite(block):
        return 2 * ((lines - block // 2) % lines) + block % 2

    return peer, start, spread, pass_on, opposite


def row_norm(tokens):
    centred = tokens - jnp.mean(tokens, axis=1, keepdims=True)
    variance = jnp.mean(centred * centred, axis=1, keepdims=True)
    inverse = lax.rsqrt(variance + 1e-06)
    return centred * inverse, inverse


def weight_grad(left, right, out, after=None):
    n_dp, shard_rows, lefts = left.shape
    step = chunk_of(lefts)
    right_rows = right[...].reshape(n_dp * shard_rows, right.shape[2])
    for i in range(lefts // step):
        cols = slice(i * step, (i + 1) * step)
        left_rows = left[:, :, cols].reshape(n_dp * shard_rows, step)
        out[cols, :] = dot(left_rows, right_rows, 0, 0).astype(BF16)
        if after is not None:
            after(i, cols)


def exchange_kernel(
    n_dp, n_mp,
    tokens_ref, cot_ref, up_hbm, down_hbm,
    rs_out, rs_grad, ncol, act, down_out,
    up_v, down_v,
    gather_n, gather_c, rs_out_send, rs_grad_send,
    ncol_send, ccol_send, ccol, hid, hid_own, act_own, slope, rows_n, rows_c,
    load_sem, own_sem, mp_send, mp_recv, dp_send, dp_recv,
):
    rows, width = tokens_ref.shape
    pieces = TILE_ROWS // rows
    wide = width // pieces
    shard_rows = rows * n_mp
    packed_rows = TILE_ROWS * n_mp
    units = up_v.shape[1]
    feats = width // n_dp

    loads = []
    parts = load_sem.shape[1]
    for w, (src, dst) in enumerate(((up_hbm, up_v), (down_hbm, down_v))):
        step = src.shape[0] // parts
        for i in range(parts):
            where = pl.ds(i * step, step)
            copy = pltpu.make_async_copy(src.at[where], dst.at[where], load_sem.at[w, i])
            copy.start()
            loads.append(copy)

    sent = []
    mp_peer, mp_start, mp_spread, mp_pass_on, mp_opposite = relay_group(
        "mp", n_mp, mp_send, mp_recv, sent
    )
    dp_peer, dp_start, dp_spread, dp_pass_on, dp_opposite = relay_group(
        "dp", n_dp, dp_send, dp_recv, sent
    )
    barrier = pltpu.get_barrier_semaphore()
    for b in range(1, n_mp):
        pl.semaphore_signal(barrier, inc=1, device_id=mp_peer(b), device_id_type=MESH)
    for b in range(1, n_dp):
        pl.semaphore_signal(barrier, inc=1, device_id=dp_peer(b), device_id_type=MESH)

    def pack(values):
        return jnp.concatenate(
            [values[:, q * wide:(q + 1) * wide] for q in range(pieces)], axis=0
        ).astype(BF16)

    xhat, _ = row_norm(tokens_ref[...].astype(F32))
    gather_n[0] = pack(xhat)
    gather_c[0] = pack(cot_ref[...].astype(F32))

    pl.semaphore_wait(barrier, n_mp - 1 + n_dp - 1)
    straight_n, crossed_n = mp_spread(0, gather_n.at[0], gather_n)
    straight_c, crossed_c = mp_spread(1, gather_c.at[0], gather_c)

    at = lax.broadcasted_iota(jnp.int32, (shard_rows, packed_rows), 0)
    to = lax.broadcasted_iota(jnp.int32, (shard_rows, packed_rows), 1)
    home = at + (at // rows) * (TILE_ROWS - rows)
    unpackers = [one_hot(to == home + q * rows) for q in range(pieces)]

    def unpack(gathered, out):
        flat = gathered[...].reshape(packed_rows, wide)
        for q in range(pieces):
            out[:, q * wide:(q + 1) * wide] = dot(unpackers[q], flat).astype(BF16)

    own = []

    def keep(src, slots, which):
        copy = pltpu.make_async_copy(src, slots.at[0], own_sem.at[which])
        copy.start()
        own.append(copy)

    def send_columns(kind, out, blocks, slots):
        for j in range(n_dp):
            blocks[j] = out[:, j * feats:(j + 1) * feats]
        got = [
            dp_start(kind, blocks.at[dp_peer(b)["dp"]], slots.at[b], b) for b in range(1, n_dp)
        ]
        keep(blocks.at[lax.axis_index("dp")], slots, kind)
        return got

    mp_pass_on(0, gather_n, straight_n, crossed_n)
    mp_pass_on(1, gather_c, straight_c, crossed_c)
    for copy in crossed_n:
        copy.wait_recv()
    unpack(gather_n, rows_n)
    got_ncol = send_columns(0, rows_n, ncol_send, ncol)

    for copy in loads[:parts]:
        copy.wait()
    step = chunk_of(units)
    for i in range(units // step):
        cols = slice(i * step, (i + 1) * step)
        pre_act = dot(rows_n[...], up_v[:, cols])
        cumulative = 0.5 * (1.0 + lax.erf(pre_act * ROOT_HALF))
        density = jnp.exp(-0.5 * pre_act * pre_act) * DENSITY_SCALE
        hid_own[:, cols] = (pre_act * cumulative).astype(BF16)
        slope[:, cols] = cumulative + pre_act * density
    straight_h, crossed_h = dp_spread(2, hid_own, hid)
    keep(hid_own, hid, 2)

    for copy in crossed_c:
        copy.wait_recv()
    unpack(gather_c, rows_c)
    got_ccol = send_columns(1, rows_c, ccol_send, ccol)

    for copy in loads[parts:]:
        copy.wait()

    def scatter(kind, partial_of, send, slots):
        total = jnp.zeros((packed_rows, wide), F32)
        for q in range(pieces):
            total += dot(unpackers[q], partial_of(q).astype(BF16), 0, 0)
        send[...] = total.astype(BF16).reshape(n_mp, TILE_ROWS, wide)
        got = [mp_start(kind, send.at[mp_opposite(b)], slots.at[b], b) for b in range(1, n_mp)]
        keep(send.at[0], slots, 2 + kind)
        return got

    got_out = scatter(
        2, lambda q: dot(hid_own[...], down_v[:, q * wide:(q + 1) * wide]), rs_out_send, rs_out
    )
    for i in range(units // step):
        cols = slice(i * step, (i + 1) * step)
        hidden_grad = dot(rows_c[...], down_v[cols, :], 1, 1)
        act_own[:, cols] = (hidden_grad * slope[:, cols]).astype(BF16)
    straight_a, crossed_a = dp_spread(3, act_own, act)
    keep(act_own, act, 3)
    got_grad = scatter(
        3, lambda q: dot(act_own[...], up_v[q * wide:(q + 1) * wide, :], 1, 1), rs_grad_send, rs_grad
    )
    dp_pass_on(2, hid, straight_h, crossed_h)
    for copy in got_ccol + crossed_h:
        copy.wait_recv()
    for copy in own:
        copy.wait()
    weight_grad(hid, ccol, down_out)
    dp_pass_on(3, act, straight_a, crossed_a)

    for copy in got_ncol + got_out + got_grad + crossed_a:
        copy.wait_recv()
    for copy in sent:
        copy.wait_send()


def result_kernel(
    tokens_ref, cot_ref, rs_out, rs_grad, ncol, act, down_out,
    mixed_ref, tgrad_ref, up_grad_hbm, down_grad_hbm,
    up_out, down_sem, up_sem,
):
    rows, width = tokens_ref.shape
    pieces = TILE_ROWS // rows
    n_mp, _, wide = rs_out.shape
    packed_rows = TILE_ROWS * n_mp
    stores = [pltpu.make_async_copy(down_out, down_grad_hbm, down_sem)]
    stores[0].start()

    def store_up(i, cols):
        copy = pltpu.make_async_copy(up_out.at[cols], up_grad_hbm.at[cols], up_sem.at[i])
        copy.start()
        stores.append(copy)

    weight_grad(ncol, act, up_out, store_up)

    at = lax.broadcasted_iota(jnp.int32, (8, packed_rows), 0)
    to = lax.broadcasted_iota(jnp.int32, (8, packed_rows), 1) % TILE_ROWS
    adders = [one_hot((to == at + q * rows) & (at < rows)) for q in range(pieces)]

    def summed(slots):
        flat = slots[...].reshape(packed_rows, wide)
        return jnp.concatenate([dot(adders[q], flat)[:rows] for q in range(pieces)], axis=1)

    tokens = tokens_ref[...].astype(F32)
    xhat, inverse = row_norm(tokens)
    mixed_ref[...] = (tokens + summed(rs_out)).astype(BF16)
    grad = summed(rs_grad)
    grad_mean = jnp.mean(grad, axis=1, keepdims=True)
    projection = jnp.mean(grad * xhat, axis=1, keepdims=True)
    tgrad_ref[...] = (
        cot_ref[...].astype(F32) + inverse * (grad - grad_mean - xhat * projection)
    ).astype(BF16)
    for copy in stores:
        copy.wait()


def body(n_dp, n_mp, tokens, cotangent, up_weight, down_weight):
    rows, width = tokens.shape
    units = up_weight.shape[1]
    feats = width // n_dp
    shard_rows = rows * n_mp
    wide = width * rows // TILE_ROWS
    packed = (n_mp, TILE_ROWS, wide)
    columns = (n_dp, shard_rows, feats)
    hiddens = (n_dp, shard_rows, units)
    in_vmem, anywhere = pl.BlockSpec(memory_space=pltpu.VMEM), pl.BlockSpec(memory_space=pl.ANY)
    exchanged = pl.pallas_call(
        functools.partial(exchange_kernel, n_dp, n_mp),
        out_shape=[
            pltpu.VMEM(shape, BF16)
            for shape in (packed, packed, columns, hiddens, (units, feats))
        ],
        in_specs=[in_vmem] * 2 + [anywhere] * 2,
        out_specs=[in_vmem] * 5,
        scratch_shapes=[
            pltpu.VMEM(up_weight.shape, BF16),
            pltpu.VMEM(down_weight.shape, BF16),
            *[pltpu.VMEM(packed, BF16)] * 4,
            *[pltpu.VMEM(columns, BF16)] * 3,
            pltpu.VMEM(hiddens, BF16),
            *[pltpu.VMEM(hiddens[1:], BF16)] * 2,
            pltpu.VMEM((shard_rows, units), F32),
            *[pltpu.VMEM((shard_rows, width), BF16)] * 2,
            pltpu.SemaphoreType.DMA((2, 4)),
            pltpu.SemaphoreType.DMA((6,)),
            pltpu.SemaphoreType.DMA((4, n_mp)),
            pltpu.SemaphoreType.DMA((4, n_mp)),
            pltpu.SemaphoreType.DMA((4, n_dp)),
            pltpu.SemaphoreType.DMA((4, n_dp)),
        ],
        compiler_params=pltpu.CompilerParams(
            collective_id=0, has_side_effects=True, vmem_limit_bytes=56 * 1024 * 1024
        ),
        cost_estimate=pl.CostEstimate(
            flops=8 * shard_rows * width * units,
            bytes_accessed=4 * width * units,
            transcendentals=2 * shard_rows * units,
        ),
    )(tokens, cotangent, up_weight, down_weight)
    return pl.pallas_call(
        result_kernel,
        out_shape=(
            jax.ShapeDtypeStruct(tokens.shape, BF16),
            jax.ShapeDtypeStruct(tokens.shape, BF16),
            jax.ShapeDtypeStruct((feats, units), BF16),
            jax.ShapeDtypeStruct((units, feats), BF16),
        ),
        in_specs=[in_vmem] * 7,
        out_specs=[in_vmem] * 2 + [anywhere] * 2,
        scratch_shapes=[
            pltpu.VMEM((feats, units), BF16),
            pltpu.SemaphoreType.DMA,
            pltpu.SemaphoreType.DMA((8,)),
        ],
        compiler_params=pltpu.CompilerParams(vmem_limit_bytes=24 * 1024 * 1024),
        cost_estimate=pl.CostEstimate(
            flops=4 * n_dp * shard_rows * units * feats,
            bytes_accessed=4 * feats * units,
            transcendentals=0,
        ),
    )(tokens, cotangent, *exchanged)


def solution(mesh):
    return jax.shard_map(
        functools.partial(body, mesh.shape["dp"], mesh.shape["mp"]),
        mesh=mesh,
        in_specs=(P(("dp", "mp"), None), P(("dp", "mp"), None), P(None, "mp"), P("mp", None)),
        out_specs=(P(("dp", "mp"), None), P(("dp", "mp"), None), P("dp", "mp"), P("mp", "dp")),
        check_vma=False,
    )
```

```python
import functools

import jax
import jax.numpy as jnp
from jax import lax
from jax.experimental import pallas as pl
from jax.experimental.pallas import tpu as pltpu
from jax.sharding import PartitionSpec as P

ROOT_HALF = 0.7071067811865476
DENSITY_SCALE = 0.3989422804014327
TILE_ROWS = 16
HALVES = 2
MESH = pl.DeviceIdType.MESH
F32 = jnp.float32
BF16 = jnp.bfloat16


def chunk_of(size, choices=(512, 384, 256)):
    for choice in choices:
        if size % choice == 0:
            return choice
    return size


def dot(left, right, left_dim=1, right_dim=0):
    return lax.dot_general(
        left, right, (((left_dim,), (right_dim,)), ((), ())), preferred_element_type=F32
    )


def one_hot(wanted):
    return jnp.where(wanted, 1.0, 0.0).astype(BF16)


def relay_group(axis, n, send_sem, recv_sem, sent):
    other_axis = "mp" if axis == "dp" else "dp"
    me, fixed = lax.axis_index(axis), lax.axis_index(other_axis)
    lines = n // 2
    line, side = me // 2, me % 2

    def peer(block):
        to_line = lax.rem(line + block // 2, lines)
        to_side = side if block % 2 == 0 else 1 - side
        return {axis: 2 * to_line + to_side, other_axis: fixed}

    def start(kind, src, dst, block, to=None):
        copy = pltpu.make_async_remote_copy(
            src_ref=src, dst_ref=dst,
            send_sem=send_sem.at[kind, block], recv_sem=recv_sem.at[kind, block],
            device_id=peer(block if to is None else to), device_id_type=MESH,
        )
        copy.start()
        sent.append(copy)
        return copy

    def spread(kind, src, slots):
        straight = [start(kind, src, slots.at[2 * k], 2 * k) for k in range(1, lines)]
        return straight, [start(kind, src, slots.at[1], 1)]

    def pass_on(kind, slots, straight, crossed):
        for k in range(1, lines):
            straight[k - 1].wait_recv()
            crossed.append(start(kind, slots.at[2 * k], slots.at[2 * k + 1], 2 * k + 1, to=1))

    def opposite(block):
        return 2 * ((lines - block // 2) % lines) + block % 2

    return peer, start, spread, pass_on, opposite


def row_norm(tokens):
    centred = tokens - jnp.mean(tokens, axis=1, keepdims=True)
    variance = jnp.mean(centred * centred, axis=1, keepdims=True)
    inverse = lax.rsqrt(variance + 1e-06)
    return centred * inverse, inverse


def weight_grad(left, right, out):
    n_dp, shard_rows, lefts = left.shape
    step = chunk_of(lefts)
    right_rows = right[...].reshape(n_dp * shard_rows, right.shape[2])
    for i in range(lefts // step):
        cols = slice(i * step, (i + 1) * step)
        left_rows = left[:, :, cols].reshape(n_dp * shard_rows, step)
        out[cols, :] = dot(left_rows, right_rows, 0, 0).astype(BF16)


def exchange_kernel(
    n_dp, n_mp,
    tokens_ref, cot_ref, up_hbm, down_hbm,
    rs_out, rs_grad, down_out, up_out,
    up_v, down_v,
    gather_n, gather_c, rs_out_send, rs_grad_send,
    ncol_send, ccol_send, ncol, ccol, hid, act, hid_own, act_own, slope, rows_n, rows_c,
    load_sem, own_sem, mp_send, mp_recv, dp_send, dp_recv,
):
    rows, width = tokens_ref.shape
    pieces = TILE_ROWS // rows
    wide = width // pieces
    shard_rows = rows * n_mp
    packed_rows = TILE_ROWS * n_mp
    units = up_v.shape[1]
    feats = width // n_dp

    loads = []
    parts = load_sem.shape[1]
    for w, (src, dst) in enumerate(((up_hbm, up_v), (down_hbm, down_v))):
        step = src.shape[0] // parts
        for i in range(parts):
            where = pl.ds(i * step, step)
            copy = pltpu.make_async_copy(src.at[where], dst.at[where], load_sem.at[w, i])
            copy.start()
            loads.append(copy)

    sent = []
    mp_peer, mp_start, mp_spread, mp_pass_on, mp_opposite = relay_group(
        "mp", n_mp, mp_send, mp_recv, sent
    )
    dp_peer, dp_start, dp_spread, dp_pass_on, dp_opposite = relay_group(
        "dp", n_dp, dp_send, dp_recv, sent
    )
    barrier = pltpu.get_barrier_semaphore()
    for b in range(1, n_mp):
        pl.semaphore_signal(barrier, inc=1, device_id=mp_peer(b), device_id_type=MESH)
    for b in range(1, n_dp):
        pl.semaphore_signal(barrier, inc=1, device_id=dp_peer(b), device_id_type=MESH)

    def pack(values):
        return jnp.concatenate(
            [values[:, q * wide:(q + 1) * wide] for q in range(pieces)], axis=0
        ).astype(BF16)

    xhat, _ = row_norm(tokens_ref[...].astype(F32))
    gather_n[0] = pack(xhat)
    gather_c[0] = pack(cot_ref[...].astype(F32))

    pl.semaphore_wait(barrier, n_mp - 1 + n_dp - 1)
    straight_n, crossed_n = mp_spread(0, gather_n.at[0], gather_n)
    straight_c, crossed_c = mp_spread(1, gather_c.at[0], gather_c)

    at = lax.broadcasted_iota(jnp.int32, (shard_rows, packed_rows), 0)
    to = lax.broadcasted_iota(jnp.int32, (shard_rows, packed_rows), 1)
    home = at + (at // rows) * (TILE_ROWS - rows)
    unpackers = [one_hot(to == home + q * rows) for q in range(pieces)]

    def unpack(gathered, out):
        flat = gathered[...].reshape(packed_rows, wide)
        for q in range(pieces):
            out[:, q * wide:(q + 1) * wide] = dot(unpackers[q], flat).astype(BF16)

    own = []

    def keep(src, slots, which):
        copy = pltpu.make_async_copy(src, slots.at[0], own_sem.at[which])
        copy.start()
        own.append(copy)

    def send_columns(kind, out, blocks, slots):
        for j in range(n_dp):
            blocks[j] = out[:, j * feats:(j + 1) * feats]
        got = [
            dp_start(kind, blocks.at[dp_peer(b)["dp"]], slots.at[b], b) for b in range(1, n_dp)
        ]
        keep(blocks.at[lax.axis_index("dp")], slots, kind)
        return got

    mp_pass_on(0, gather_n, straight_n, crossed_n)
    mp_pass_on(1, gather_c, straight_c, crossed_c)
    for copy in crossed_n:
        copy.wait_recv()
    unpack(gather_n, rows_n)
    got_ncol = send_columns(0, rows_n, ncol_send, ncol)

    for copy in loads[:parts]:
        copy.wait()
    step = chunk_of(units)
    for i in range(units // step):
        cols = slice(i * step, (i + 1) * step)
        pre_act = dot(rows_n[...], up_v[:, cols])
        cumulative = 0.5 * (1.0 + lax.erf(pre_act * ROOT_HALF))
        density = jnp.exp(-0.5 * pre_act * pre_act) * DENSITY_SCALE
        hid_own[:, cols] = (pre_act * cumulative).astype(BF16)
        slope[:, cols] = cumulative + pre_act * density
    straight_h, crossed_h = dp_spread(2, hid_own, hid)
    keep(hid_own, hid, 2)

    for copy in crossed_c:
        copy.wait_recv()
    unpack(gather_c, rows_c)
    got_ccol = send_columns(1, rows_c, ccol_send, ccol)

    for copy in loads[parts:]:
        copy.wait()

    half = wide // HALVES

    def scatter(kind, partial_of, send, slots):
        got = []
        for h in range(HALVES):
            partial = partial_of(slice(h * pieces * half, (h + 1) * pieces * half)).astype(BF16)
            total = jnp.zeros((packed_rows, half), F32)
            for q in range(pieces):
                total += dot(unpackers[q], partial[:, q * half:(q + 1) * half], 0, 0)
            send[h] = total.astype(BF16).reshape(n_mp, TILE_ROWS, half)
            got += [
                mp_start(kind + h, send.at[h, mp_opposite(b)], slots.at[h, b], b)
                for b in range(1, n_mp)
            ]
            keep(send.at[h, 0], slots.at[h], 2 + kind + h)
        return got

    for i in range(units // step):
        cols = slice(i * step, (i + 1) * step)
        hidden_grad = dot(rows_c[...], down_v[cols, :], 1, 1)
        act_own[:, cols] = (hidden_grad * slope[:, cols]).astype(BF16)
    straight_a, crossed_a = dp_spread(3, act_own, act)
    keep(act_own, act, 3)
    got_grad = scatter(
        2 + HALVES, lambda cols: dot(act_own[...], up_v[cols, :], 1, 1), rs_grad_send, rs_grad
    )
    dp_pass_on(2, hid, straight_h, crossed_h)
    got_out = scatter(2, lambda cols: dot(hid_own[...], down_v[:, cols]), rs_out_send, rs_out)
    dp_pass_on(3, act, straight_a, crossed_a)
    for copy in got_ccol + crossed_h:
        copy.wait_recv()
    for copy in own:
        copy.wait()
    weight_grad(hid, ccol, down_out)
    for copy in got_ncol + crossed_a:
        copy.wait_recv()
    weight_grad(ncol, act, up_out)
    for copy in got_grad + got_out:
        copy.wait_recv()
    for copy in sent:
        copy.wait_send()


def result_kernel(
    tokens_ref, cot_ref, rs_out, rs_grad, down_out, up_out,
    mixed_ref, tgrad_ref, up_grad_hbm, down_grad_hbm,
    store_sem,
):
    rows, width = tokens_ref.shape
    pieces = TILE_ROWS // rows
    _, n_mp, _, half = rs_out.shape
    packed_rows = TILE_ROWS * n_mp
    stores = [
        pltpu.make_async_copy(down_out, down_grad_hbm, store_sem.at[0]),
        pltpu.make_async_copy(up_out, up_grad_hbm, store_sem.at[1]),
    ]
    for copy in stores:
        copy.start()

    at = lax.broadcasted_iota(jnp.int32, (8, packed_rows), 0)
    to = lax.broadcasted_iota(jnp.int32, (8, packed_rows), 1) % TILE_ROWS
    adders = [one_hot((to == at + q * rows) & (at < rows)) for q in range(pieces)]

    def summed(slots):
        flats = [slots[h].reshape(packed_rows, half) for h in range(HALVES)]
        return jnp.concatenate(
            [dot(adders[q], flat)[:rows] for flat in flats for q in range(pieces)], axis=1
        )

    tokens = tokens_ref[...].astype(F32)
    xhat, inverse = row_norm(tokens)
    mixed_ref[...] = (tokens + summed(rs_out)).astype(BF16)
    grad = summed(rs_grad)
    grad_mean = jnp.mean(grad, axis=1, keepdims=True)
    projection = jnp.mean(grad * xhat, axis=1, keepdims=True)
    tgrad_ref[...] = (
        cot_ref[...].astype(F32) + inverse * (grad - grad_mean - xhat * projection)
    ).astype(BF16)
    for copy in stores:
        copy.wait()


def body(n_dp, n_mp, tokens, cotangent, up_weight, down_weight):
    rows, width = tokens.shape
    units = up_weight.shape[1]
    feats = width // n_dp
    shard_rows = rows * n_mp
    wide = width * rows // TILE_ROWS
    packed = (n_mp, TILE_ROWS, wide)
    scattered = (HALVES, n_mp, TILE_ROWS, wide // HALVES)
    columns = (n_dp, shard_rows, feats)
    hiddens = (n_dp, shard_rows, units)
    in_vmem, anywhere = pl.BlockSpec(memory_space=pltpu.VMEM), pl.BlockSpec(memory_space=pl.ANY)
    exchanged = pl.pallas_call(
        functools.partial(exchange_kernel, n_dp, n_mp),
        out_shape=[
            pltpu.VMEM(shape, BF16)
            for shape in (scattered, scattered, (units, feats), (feats, units))
        ],
        in_specs=[in_vmem] * 2 + [anywhere] * 2,
        out_specs=[in_vmem] * 4,
        scratch_shapes=[
            pltpu.VMEM(up_weight.shape, BF16),
            pltpu.VMEM(down_weight.shape, BF16),
            *[pltpu.VMEM(packed, BF16)] * 2,
            *[pltpu.VMEM(scattered, BF16)] * 2,
            *[pltpu.VMEM(columns, BF16)] * 4,
            *[pltpu.VMEM(hiddens, BF16)] * 2,
            *[pltpu.VMEM(hiddens[1:], BF16)] * 2,
            pltpu.VMEM((shard_rows, units), F32),
            *[pltpu.VMEM((shard_rows, width), BF16)] * 2,
            pltpu.SemaphoreType.DMA((2, 4)),
            pltpu.SemaphoreType.DMA((4 + 2 * HALVES,)),
            pltpu.SemaphoreType.DMA((2 + 2 * HALVES, n_mp)),
            pltpu.SemaphoreType.DMA((2 + 2 * HALVES, n_mp)),
            pltpu.SemaphoreType.DMA((4, n_dp)),
            pltpu.SemaphoreType.DMA((4, n_dp)),
        ],
        compiler_params=pltpu.CompilerParams(
            collective_id=0, has_side_effects=True, vmem_limit_bytes=56 * 1024 * 1024
        ),
        cost_estimate=pl.CostEstimate(
            flops=8 * shard_rows * width * units,
            bytes_accessed=4 * width * units,
            transcendentals=2 * shard_rows * units,
        ),
    )(tokens, cotangent, up_weight, down_weight)
    return pl.pallas_call(
        result_kernel,
        out_shape=(
            jax.ShapeDtypeStruct(tokens.shape, BF16),
            jax.ShapeDtypeStruct(tokens.shape, BF16),
            jax.ShapeDtypeStruct((feats, units), BF16),
            jax.ShapeDtypeStruct((units, feats), BF16),
        ),
        in_specs=[in_vmem] * 6,
        out_specs=[in_vmem] * 2 + [anywhere] * 2,
        scratch_shapes=[pltpu.SemaphoreType.DMA((2,))],
        compiler_params=pltpu.CompilerParams(vmem_limit_bytes=24 * 1024 * 1024),
        cost_estimate=pl.CostEstimate(
            flops=0,
            bytes_accessed=4 * feats * units,
            transcendentals=0,
        ),
    )(tokens, cotangent, *exchanged)


def solution(mesh):
    return jax.shard_map(
        functools.partial(body, mesh.shape["dp"], mesh.shape["mp"]),
        mesh=mesh,
        in_specs=(P(("dp", "mp"), None), P(("dp", "mp"), None), P(None, "mp"), P("mp", None)),
        out_specs=(P(("dp", "mp"), None), P(("dp", "mp"), None), P("dp", "mp"), P("mp", "dp")),
        check_vma=False,
    )
```

```python
import functools

import jax
import jax.numpy as jnp
from jax import lax
from jax.experimental import pallas as pl
from jax.experimental.pallas import tpu as pltpu
from jax.sharding import PartitionSpec as P

ROOT_HALF = 0.7071067811865476
DENSITY_SCALE = 0.3989422804014327
TILE_ROWS = 16
HALVES = 1
MESH = pl.DeviceIdType.MESH
F32 = jnp.float32
BF16 = jnp.bfloat16


def chunk_of(size, choices=(512, 384, 256)):
    for choice in choices:
        if size % choice == 0:
            return choice
    return size


def dot(left, right, left_dim=1, right_dim=0):
    return lax.dot_general(
        left, right, (((left_dim,), (right_dim,)), ((), ())), preferred_element_type=F32
    )


def one_hot(wanted):
    return jnp.where(wanted, 1.0, 0.0).astype(BF16)


def relay_group(axis, n, send_sem, recv_sem, sent):
    other_axis = "mp" if axis == "dp" else "dp"
    me, fixed = lax.axis_index(axis), lax.axis_index(other_axis)
    lines = n // 2
    line, side = me // 2, me % 2

    def peer(block):
        to_line = lax.rem(line + block // 2, lines)
        to_side = side if block % 2 == 0 else 1 - side
        return {axis: 2 * to_line + to_side, other_axis: fixed}

    def start(kind, src, dst, block, to=None):
        copy = pltpu.make_async_remote_copy(
            src_ref=src, dst_ref=dst,
            send_sem=send_sem.at[kind, block], recv_sem=recv_sem.at[kind, block],
            device_id=peer(block if to is None else to), device_id_type=MESH,
        )
        copy.start()
        sent.append(copy)
        return copy

    def spread(kind, src, slots):
        straight = [start(kind, src, slots.at[2 * k], 2 * k) for k in range(1, lines)]
        return straight, [start(kind, src, slots.at[1], 1)]

    def pass_on(kind, slots, straight, crossed):
        for k in range(1, lines):
            straight[k - 1].wait_recv()
            crossed.append(start(kind, slots.at[2 * k], slots.at[2 * k + 1], 2 * k + 1, to=1))

    def opposite(block):
        return 2 * ((lines - block // 2) % lines) + block % 2

    return peer, start, spread, pass_on, opposite


def row_norm(tokens):
    centred = tokens - jnp.mean(tokens, axis=1, keepdims=True)
    variance = jnp.mean(centred * centred, axis=1, keepdims=True)
    inverse = lax.rsqrt(variance + 1e-06)
    return centred * inverse, inverse


def weight_grad(left, right, out, after=None):
    n_dp, shard_rows, lefts = left.shape
    step = chunk_of(lefts)
    right_rows = right[...].reshape(n_dp * shard_rows, right.shape[2])
    for i in range(lefts // step):
        cols = slice(i * step, (i + 1) * step)
        left_rows = left[:, :, cols].reshape(n_dp * shard_rows, step)
        out[cols, :] = dot(left_rows, right_rows, 0, 0).astype(BF16)
        if after is not None:
            after(i, cols)


def exchange_kernel(
    n_dp, n_mp,
    tokens_ref, cot_ref, up_hbm, down_hbm,
    rs_out, rs_grad, ncol, act, down_out,
    up_v, down_v,
    gather_n, gather_c, rs_out_send, rs_grad_send,
    ncol_send, ccol_send, ccol, hid, hid_own, act_own, slope, rows_n, rows_c,
    load_sem, own_sem, mp_send, mp_recv, dp_send, dp_recv,
):
    rows, width = tokens_ref.shape
    pieces = TILE_ROWS // rows
    wide = width // pieces
    shard_rows = rows * n_mp
    packed_rows = TILE_ROWS * n_mp
    units = up_v.shape[1]
    feats = width // n_dp

    loads = []
    parts = load_sem.shape[1]
    for w, (src, dst) in enumerate(((up_hbm, up_v), (down_hbm, down_v))):
        step = src.shape[0] // parts
        for i in range(parts):
            where = pl.ds(i * step, step)
            copy = pltpu.make_async_copy(src.at[where], dst.at[where], load_sem.at[w, i])
            copy.start()
            loads.append(copy)

    sent = []
    mp_peer, mp_start, mp_spread, mp_pass_on, mp_opposite = relay_group(
        "mp", n_mp, mp_send, mp_recv, sent
    )
    dp_peer, dp_start, dp_spread, dp_pass_on, dp_opposite = relay_group(
        "dp", n_dp, dp_send, dp_recv, sent
    )
    barrier = pltpu.get_barrier_semaphore()
    for b in range(1, n_mp):
        pl.semaphore_signal(barrier, inc=1, device_id=mp_peer(b), device_id_type=MESH)
    for b in range(1, n_dp):
        pl.semaphore_signal(barrier, inc=1, device_id=dp_peer(b), device_id_type=MESH)

    def pack(values):
        return jnp.concatenate(
            [values[:, q * wide:(q + 1) * wide] for q in range(pieces)], axis=0
        ).astype(BF16)

    xhat, _ = row_norm(tokens_ref[...].astype(F32))
    gather_n[0] = pack(xhat)
    gather_c[0] = pack(cot_ref[...].astype(F32))

    pl.semaphore_wait(barrier, n_mp - 1 + n_dp - 1)
    straight_n, crossed_n = mp_spread(0, gather_n.at[0], gather_n)
    straight_c, crossed_c = mp_spread(1, gather_c.at[0], gather_c)

    def home(packed):
        return packed % TILE_ROWS // rows * shard_rows + packed // TILE_ROWS * rows + packed % rows

    square = (packed_rows, packed_rows)
    first = lax.broadcasted_iota(jnp.int32, square, 0)
    second = lax.broadcasted_iota(jnp.int32, square, 1)
    packer = one_hot(second == home(first))
    unpacker = one_hot(first == home(second))

    def unpack(gathered, out):
        flat = dot(unpacker, gathered[...].reshape(packed_rows, wide)).astype(BF16)
        for q in range(pieces):
            out[:, q * wide:(q + 1) * wide] = flat[q * shard_rows:(q + 1) * shard_rows]

    own = []

    def keep(src, slots, which):
        copy = pltpu.make_async_copy(src, slots.at[0], own_sem.at[which])
        copy.start()
        own.append(copy)

    def send_columns(kind, out, blocks, slots):
        for j in range(n_dp):
            blocks[j] = out[:, j * feats:(j + 1) * feats]
        got = [
            dp_start(kind, blocks.at[dp_peer(b)["dp"]], slots.at[b], b) for b in range(1, n_dp)
        ]
        keep(blocks.at[lax.axis_index("dp")], slots, kind)
        return got

    mp_pass_on(0, gather_n, straight_n, crossed_n)
    mp_pass_on(1, gather_c, straight_c, crossed_c)
    for copy in crossed_n:
        copy.wait_recv()
    unpack(gather_n, rows_n)
    got_ncol = send_columns(0, rows_n, ncol_send, ncol)

    for copy in loads[:parts]:
        copy.wait()
    step = chunk_of(units)
    for i in range(units // step):
        cols = slice(i * step, (i + 1) * step)
        pre_act = dot(rows_n[...], up_v[:, cols])
        cumulative = 0.5 * (1.0 + lax.erf(pre_act * ROOT_HALF))
        density = jnp.exp(-0.5 * pre_act * pre_act) * DENSITY_SCALE
        hid_own[:, cols] = (pre_act * cumulative).astype(BF16)
        slope[:, cols] = cumulative + pre_act * density
    straight_h, crossed_h = dp_spread(2, hid_own, hid)
    keep(hid_own, hid, 2)

    for copy in crossed_c:
        copy.wait_recv()
    unpack(gather_c, rows_c)
    got_ccol = send_columns(1, rows_c, ccol_send, ccol)

    for copy in loads[parts:]:
        copy.wait()

    half = wide // HALVES

    def scatter(kind, partial_of, send, slots):
        got = []
        for h in range(HALVES):
            partial = partial_of(slice(h * pieces * half, (h + 1) * pieces * half)).astype(BF16)
            stacked = jnp.concatenate(
                [partial[:, q * half:(q + 1) * half] for q in range(pieces)], axis=0
            )
            total = dot(packer, stacked)
            send[h] = total.astype(BF16).reshape(n_mp, TILE_ROWS, half)
            got += [
                mp_start(kind + h, send.at[h, mp_opposite(b)], slots.at[h, b], b)
                for b in range(1, n_mp)
            ]
            keep(send.at[h, 0], slots.at[h], 2 + kind + h)
        return got

    for i in range(units // step):
        cols = slice(i * step, (i + 1) * step)
        hidden_grad = dot(rows_c[...], down_v[cols, :], 1, 1)
        act_own[:, cols] = (hidden_grad * slope[:, cols]).astype(BF16)
    straight_a, crossed_a = dp_spread(3, act_own, act)
    keep(act_own, act, 3)
    got_grad = scatter(
        2 + HALVES, lambda cols: dot(act_own[...], up_v[cols, :], 1, 1), rs_grad_send, rs_grad
    )
    dp_pass_on(2, hid, straight_h, crossed_h)
    got_out = scatter(2, lambda cols: dot(hid_own[...], down_v[:, cols]), rs_out_send, rs_out)
    dp_pass_on(3, act, straight_a, crossed_a)
    for copy in got_ccol + crossed_h:
        copy.wait_recv()
    for copy in own:
        copy.wait()
    weight_grad(hid, ccol, down_out)
    for copy in got_ncol + crossed_a:
        copy.wait_recv()
    for copy in got_grad + got_out:
        copy.wait_recv()
    for copy in sent:
        copy.wait_send()


def result_kernel(
    tokens_ref, cot_ref, rs_out, rs_grad, ncol, act, down_out,
    mixed_ref, tgrad_ref, up_grad_hbm, down_grad_hbm,
    up_out, down_sem, up_sem,
):
    rows, width = tokens_ref.shape
    pieces = TILE_ROWS // rows
    _, n_mp, _, half = rs_out.shape
    packed_rows = TILE_ROWS * n_mp
    stores = []

    def store(out, out_hbm, cols, sem):
        copy = pltpu.make_async_copy(out.at[cols], out_hbm.at[cols], sem)
        copy.start()
        stores.append(copy)

    parts = down_sem.shape[0]
    step = down_out.shape[0] // parts
    for i in range(parts):
        store(down_out, down_grad_hbm, slice(i * step, (i + 1) * step), down_sem.at[i])
    weight_grad(ncol, act, up_out, lambda i, cols: store(up_out, up_grad_hbm, cols, up_sem.at[i]))

    at = lax.broadcasted_iota(jnp.int32, (8, packed_rows), 0)
    to = lax.broadcasted_iota(jnp.int32, (8, packed_rows), 1) % TILE_ROWS
    adders = [one_hot((to == at + q * rows) & (at < rows)) for q in range(pieces)]

    def summed(slots):
        flats = [slots[h].reshape(packed_rows, half) for h in range(HALVES)]
        return jnp.concatenate(
            [dot(adders[q], flat)[:rows] for flat in flats for q in range(pieces)], axis=1
        )

    tokens = tokens_ref[...].astype(F32)
    xhat, inverse = row_norm(tokens)
    mixed_ref[...] = (tokens + summed(rs_out)).astype(BF16)
    grad = summed(rs_grad)
    grad_mean = jnp.mean(grad, axis=1, keepdims=True)
    projection = jnp.mean(grad * xhat, axis=1, keepdims=True)
    tgrad_ref[...] = (
        cot_ref[...].astype(F32) + inverse * (grad - grad_mean - xhat * projection)
    ).astype(BF16)
    for copy in stores:
        copy.wait()


def body(n_dp, n_mp, tokens, cotangent, up_weight, down_weight):
    rows, width = tokens.shape
    units = up_weight.shape[1]
    feats = width // n_dp
    shard_rows = rows * n_mp
    wide = width * rows // TILE_ROWS
    packed = (n_mp, TILE_ROWS, wide)
    scattered = (HALVES, n_mp, TILE_ROWS, wide // HALVES)
    columns = (n_dp, shard_rows, feats)
    hiddens = (n_dp, shard_rows, units)
    in_vmem, anywhere = pl.BlockSpec(memory_space=pltpu.VMEM), pl.BlockSpec(memory_space=pl.ANY)
    exchanged = pl.pallas_call(
        functools.partial(exchange_kernel, n_dp, n_mp),
        out_shape=[
            pltpu.VMEM(shape, BF16)
            for shape in (scattered, scattered, columns, hiddens, (units, feats))
        ],
        in_specs=[in_vmem] * 2 + [anywhere] * 2,
        out_specs=[in_vmem] * 5,
        scratch_shapes=[
            pltpu.VMEM(up_weight.shape, BF16),
            pltpu.VMEM(down_weight.shape, BF16),
            *[pltpu.VMEM(packed, BF16)] * 2,
            *[pltpu.VMEM(scattered, BF16)] * 2,
            *[pltpu.VMEM(columns, BF16)] * 3,
            pltpu.VMEM(hiddens, BF16),
            *[pltpu.VMEM(hiddens[1:], BF16)] * 2,
            pltpu.VMEM((shard_rows, units), F32),
            *[pltpu.VMEM((shard_rows, width), BF16)] * 2,
            pltpu.SemaphoreType.DMA((2, 4)),
            pltpu.SemaphoreType.DMA((4 + 2 * HALVES,)),
            pltpu.SemaphoreType.DMA((2 + 2 * HALVES, n_mp)),
            pltpu.SemaphoreType.DMA((2 + 2 * HALVES, n_mp)),
            pltpu.SemaphoreType.DMA((4, n_dp)),
            pltpu.SemaphoreType.DMA((4, n_dp)),
        ],
        compiler_params=pltpu.CompilerParams(
            collective_id=0, has_side_effects=True, vmem_limit_bytes=56 * 1024 * 1024
        ),
        cost_estimate=pl.CostEstimate(
            flops=8 * shard_rows * width * units,
            bytes_accessed=4 * width * units,
            transcendentals=2 * shard_rows * units,
        ),
    )(tokens, cotangent, up_weight, down_weight)
    return pl.pallas_call(
        result_kernel,
        out_shape=(
            jax.ShapeDtypeStruct(tokens.shape, BF16),
            jax.ShapeDtypeStruct(tokens.shape, BF16),
            jax.ShapeDtypeStruct((feats, units), BF16),
            jax.ShapeDtypeStruct((units, feats), BF16),
        ),
        in_specs=[in_vmem] * 7,
        out_specs=[in_vmem] * 2 + [anywhere] * 2,
        scratch_shapes=[
            pltpu.VMEM((feats, units), BF16),
            pltpu.SemaphoreType.DMA((4,)),
            pltpu.SemaphoreType.DMA((8,)),
        ],
        compiler_params=pltpu.CompilerParams(vmem_limit_bytes=24 * 1024 * 1024),
        cost_estimate=pl.CostEstimate(
            flops=2 * n_dp * shard_rows * units * feats,
            bytes_accessed=4 * feats * units,
            transcendentals=0,
        ),
    )(tokens, cotangent, *exchanged)


def solution(mesh):
    return jax.shard_map(
        functools.partial(body, mesh.shape["dp"], mesh.shape["mp"]),
        mesh=mesh,
        in_specs=(P(("dp", "mp"), None), P(("dp", "mp"), None), P(None, "mp"), P("mp", None)),
        out_specs=(P(("dp", "mp"), None), P(("dp", "mp"), None), P("dp", "mp"), P("mp", "dp")),
        check_vma=False,
    )
```

```python
import functools

import jax
import jax.numpy as jnp
from jax import lax
from jax.experimental import pallas as pl
from jax.experimental.pallas import tpu as pltpu
from jax.sharding import PartitionSpec as P

ROOT_HALF = 0.7071067811865476
DENSITY_SCALE = 0.3989422804014327
TILE_ROWS = 16
HALVES = 1
MESH = pl.DeviceIdType.MESH
F32 = jnp.float32
BF16 = jnp.bfloat16


def chunk_of(size, choices=(512, 384, 256)):
    for choice in choices:
        if size % choice == 0:
            return choice
    return size


def dot(left, right, left_dim=1, right_dim=0):
    return lax.dot_general(
        left, right, (((left_dim,), (right_dim,)), ((), ())), preferred_element_type=F32
    )


def one_hot(wanted):
    return jnp.where(wanted, 1.0, 0.0).astype(BF16)


def relay_group(axis, n, send_sem, recv_sem, sent):
    other_axis = "mp" if axis == "dp" else "dp"
    me, fixed = lax.axis_index(axis), lax.axis_index(other_axis)
    lines = n // 2
    line, side = me // 2, me % 2

    def peer(block):
        to_line = lax.rem(line + block // 2, lines)
        to_side = side if block % 2 == 0 else 1 - side
        return {axis: 2 * to_line + to_side, other_axis: fixed}

    def start(kind, src, dst, block, to=None):
        copy = pltpu.make_async_remote_copy(
            src_ref=src, dst_ref=dst,
            send_sem=send_sem.at[kind, block], recv_sem=recv_sem.at[kind, block],
            device_id=peer(block if to is None else to), device_id_type=MESH,
        )
        copy.start()
        sent.append(copy)
        return copy

    def spread(kind, src, slots):
        straight = [start(kind, src, slots.at[2 * k], 2 * k) for k in range(1, lines)]
        return straight, [start(kind, src, slots.at[1], 1)]

    def pass_on(kind, slots, straight, crossed):
        for k in range(1, lines):
            straight[k - 1].wait_recv()
            crossed.append(start(kind, slots.at[2 * k], slots.at[2 * k + 1], 2 * k + 1, to=1))

    def opposite(block):
        return 2 * ((lines - block // 2) % lines) + block % 2

    return peer, start, spread, pass_on, opposite


def row_norm(tokens):
    centred = tokens - jnp.mean(tokens, axis=1, keepdims=True)
    variance = jnp.mean(centred * centred, axis=1, keepdims=True)
    inverse = lax.rsqrt(variance + 1e-06)
    return centred * inverse, inverse


def weight_grad(left, right, out, after=None):
    n_dp, shard_rows, lefts = left.shape
    step = chunk_of(lefts)
    right_rows = right[...].reshape(n_dp * shard_rows, right.shape[2])
    for i in range(lefts // step):
        cols = slice(i * step, (i + 1) * step)
        left_rows = left[:, :, cols].reshape(n_dp * shard_rows, step)
        out[cols, :] = dot(left_rows, right_rows, 0, 0).astype(BF16)
        if after is not None:
            after(i, cols)


def exchange_kernel(
    n_dp, n_mp,
    tokens_ref, cot_ref, up_hbm, down_hbm,
    rs_out, rs_grad, ncol, act, down_out,
    up_v, down_v,
    gather_n, gather_c, rs_out_send, rs_grad_send,
    ncol_send, ccol_send, ccol, hid, hid_own, act_own, slope, rows_n, rows_c,
    load_sem, own_sem, mp_send, mp_recv, dp_send, dp_recv,
):
    rows, width = tokens_ref.shape
    pieces = TILE_ROWS // rows
    wide = width // pieces
    shard_rows = rows * n_mp
    packed_rows = TILE_ROWS * n_mp
    units = up_v.shape[1]
    feats = width // n_dp

    loads = []
    parts = load_sem.shape[1]
    for w, (src, dst) in enumerate(((up_hbm, up_v), (down_hbm, down_v))):
        step = src.shape[0] // parts
        for i in range(parts):
            where = pl.ds(i * step, step)
            copy = pltpu.make_async_copy(src.at[where], dst.at[where], load_sem.at[w, i])
            copy.start()
            loads.append(copy)

    sent = []
    mp_peer, mp_start, mp_spread, mp_pass_on, mp_opposite = relay_group(
        "mp", n_mp, mp_send, mp_recv, sent
    )
    dp_peer, dp_start, dp_spread, dp_pass_on, dp_opposite = relay_group(
        "dp", n_dp, dp_send, dp_recv, sent
    )
    barrier = pltpu.get_barrier_semaphore()
    for b in range(1, n_mp):
        pl.semaphore_signal(barrier, inc=1, device_id=mp_peer(b), device_id_type=MESH)
    for b in range(1, n_dp):
        pl.semaphore_signal(barrier, inc=1, device_id=dp_peer(b), device_id_type=MESH)

    def pack(values):
        return jnp.concatenate(
            [values[:, q * wide:(q + 1) * wide] for q in range(pieces)], axis=0
        ).astype(BF16)

    xhat, _ = row_norm(tokens_ref[...].astype(F32))
    gather_n[0] = pack(xhat)
    gather_c[0] = pack(cot_ref[...].astype(F32))

    pl.semaphore_wait(barrier, n_mp - 1 + n_dp - 1)
    straight_n, crossed_n = mp_spread(0, gather_n.at[0], gather_n)
    straight_c, crossed_c = mp_spread(1, gather_c.at[0], gather_c)

    def home(packed):
        return packed % TILE_ROWS // rows * shard_rows + packed // TILE_ROWS * rows + packed % rows

    square = (packed_rows, packed_rows)
    first = lax.broadcasted_iota(jnp.int32, square, 0)
    second = lax.broadcasted_iota(jnp.int32, square, 1)
    packer = one_hot(second == home(first))
    unpacker = one_hot(first == home(second))

    def unpack(gathered, out):
        flat = dot(unpacker, gathered[...].reshape(packed_rows, wide)).astype(BF16)
        for q in range(pieces):
            out[:, q * wide:(q + 1) * wide] = flat[q * shard_rows:(q + 1) * shard_rows]

    own = []

    def keep(src, slots, which):
        copy = pltpu.make_async_copy(src, slots.at[0], own_sem.at[which])
        copy.start()
        own.append(copy)

    def send_columns(kind, out, blocks, slots):
        for j in range(n_dp):
            blocks[j] = out[:, j * feats:(j + 1) * feats]
        got = [
            dp_start(kind, blocks.at[dp_peer(b)["dp"]], slots.at[b], b) for b in range(1, n_dp)
        ]
        keep(blocks.at[lax.axis_index("dp")], slots, kind)
        return got

    mp_pass_on(0, gather_n, straight_n, crossed_n)
    mp_pass_on(1, gather_c, straight_c, crossed_c)
    for copy in crossed_n:
        copy.wait_recv()
    unpack(gather_n, rows_n)
    got_ncol = send_columns(0, rows_n, ncol_send, ncol)

    for copy in loads[:parts]:
        copy.wait()
    step = chunk_of(units)
    for i in range(units // step):
        cols = slice(i * step, (i + 1) * step)
        pre_act = dot(rows_n[...], up_v[:, cols])
        cumulative = 0.5 * (1.0 + lax.erf(pre_act * ROOT_HALF))
        density = jnp.exp(-0.5 * pre_act * pre_act) * DENSITY_SCALE
        hid_own[:, cols] = (pre_act * cumulative).astype(BF16)
        slope[:, cols] = cumulative + pre_act * density
    straight_h, crossed_h = dp_spread(2, hid_own, hid)
    keep(hid_own, hid, 2)

    for copy in crossed_c:
        copy.wait_recv()
    unpack(gather_c, rows_c)
    got_ccol = send_columns(1, rows_c, ccol_send, ccol)

    for copy in loads[parts:]:
        copy.wait()

    half = wide // HALVES

    def scatter(kind, partial_of, send, slots):
        got = []
        for h in range(HALVES):
            partial = partial_of(slice(h * pieces * half, (h + 1) * pieces * half)).astype(BF16)
            stacked = jnp.concatenate(
                [partial[:, q * half:(q + 1) * half] for q in range(pieces)], axis=0
            )
            total = dot(packer, stacked)
            send[h] = total.astype(BF16).reshape(n_mp, TILE_ROWS, half)
            got += [
                mp_start(kind + h, send.at[h, mp_opposite(b)], slots.at[h, b], b)
                for b in range(1, n_mp)
            ]
            keep(send.at[h, 0], slots.at[h], 2 + kind + h)
        return got

    got_out = scatter(2, lambda cols: dot(hid_own[...], down_v[:, cols]), rs_out_send, rs_out)
    for i in range(units // step):
        cols = slice(i * step, (i + 1) * step)
        hidden_grad = dot(rows_c[...], down_v[cols, :], 1, 1)
        act_own[:, cols] = (hidden_grad * slope[:, cols]).astype(BF16)
    straight_a, crossed_a = dp_spread(3, act_own, act)
    keep(act_own, act, 3)
    got_grad = scatter(
        2 + HALVES, lambda cols: dot(act_own[...], up_v[cols, :], 1, 1), rs_grad_send, rs_grad
    )
    dp_pass_on(2, hid, straight_h, crossed_h)
    dp_pass_on(3, act, straight_a, crossed_a)
    for copy in got_ccol + crossed_h:
        copy.wait_recv()
    for copy in own:
        copy.wait()
    weight_grad(hid, ccol, down_out)
    for copy in got_ncol + crossed_a:
        copy.wait_recv()
    for copy in got_grad + got_out:
        copy.wait_recv()
    for copy in sent:
        copy.wait_send()


def result_kernel(
    tokens_ref, cot_ref, rs_out, rs_grad, ncol, act, down_out,
    mixed_ref, tgrad_ref, up_grad_hbm, down_grad_hbm,
    up_out, down_sem, up_sem,
):
    rows, width = tokens_ref.shape
    pieces = TILE_ROWS // rows
    _, n_mp, _, half = rs_out.shape
    packed_rows = TILE_ROWS * n_mp
    stores = []

    def store(out, out_hbm, cols, sem):
        copy = pltpu.make_async_copy(out.at[cols], out_hbm.at[cols], sem)
        copy.start()
        stores.append(copy)

    parts = down_sem.shape[0]
    step = down_out.shape[0] // parts
    for i in range(parts):
        store(down_out, down_grad_hbm, slice(i * step, (i + 1) * step), down_sem.at[i])
    weight_grad(ncol, act, up_out, lambda i, cols: store(up_out, up_grad_hbm, cols, up_sem.at[i]))

    at = lax.broadcasted_iota(jnp.int32, (8, packed_rows), 0)
    to = lax.broadcasted_iota(jnp.int32, (8, packed_rows), 1) % TILE_ROWS
    adders = [one_hot((to == at + q * rows) & (at < rows)) for q in range(pieces)]

    def summed(slots):
        flats = [slots[h].reshape(packed_rows, half) for h in range(HALVES)]
        return jnp.concatenate(
            [dot(adders[q], flat)[:rows] for flat in flats for q in range(pieces)], axis=1
        )

    tokens = tokens_ref[...].astype(F32)
    xhat, inverse = row_norm(tokens)
    mixed_ref[...] = (tokens + summed(rs_out)).astype(BF16)
    grad = summed(rs_grad)
    grad_mean = jnp.mean(grad, axis=1, keepdims=True)
    projection = jnp.mean(grad * xhat, axis=1, keepdims=True)
    tgrad_ref[...] = (
        cot_ref[...].astype(F32) + inverse * (grad - grad_mean - xhat * projection)
    ).astype(BF16)
    for copy in stores:
        copy.wait()


def body(n_dp, n_mp, tokens, cotangent, up_weight, down_weight):
    rows, width = tokens.shape
    units = up_weight.shape[1]
    feats = width // n_dp
    shard_rows = rows * n_mp
    wide = width * rows // TILE_ROWS
    packed = (n_mp, TILE_ROWS, wide)
    scattered = (HALVES, n_mp, TILE_ROWS, wide // HALVES)
    columns = (n_dp, shard_rows, feats)
    hiddens = (n_dp, shard_rows, units)
    in_vmem, anywhere = pl.BlockSpec(memory_space=pltpu.VMEM), pl.BlockSpec(memory_space=pl.ANY)
    exchanged = pl.pallas_call(
        functools.partial(exchange_kernel, n_dp, n_mp),
        out_shape=[
            pltpu.VMEM(shape, BF16)
            for shape in (scattered, scattered, columns, hiddens, (units, feats))
        ],
        in_specs=[in_vmem] * 2 + [anywhere] * 2,
        out_specs=[in_vmem] * 5,
        scratch_shapes=[
            pltpu.VMEM(up_weight.shape, BF16),
            pltpu.VMEM(down_weight.shape, BF16),
            *[pltpu.VMEM(packed, BF16)] * 2,
            *[pltpu.VMEM(scattered, BF16)] * 2,
            *[pltpu.VMEM(columns, BF16)] * 3,
            pltpu.VMEM(hiddens, BF16),
            *[pltpu.VMEM(hiddens[1:], BF16)] * 2,
            pltpu.VMEM((shard_rows, units), F32),
            *[pltpu.VMEM((shard_rows, width), BF16)] * 2,
            pltpu.SemaphoreType.DMA((2, 4)),
            pltpu.SemaphoreType.DMA((4 + 2 * HALVES,)),
            pltpu.SemaphoreType.DMA((2 + 2 * HALVES, n_mp)),
            pltpu.SemaphoreType.DMA((2 + 2 * HALVES, n_mp)),
            pltpu.SemaphoreType.DMA((4, n_dp)),
            pltpu.SemaphoreType.DMA((4, n_dp)),
        ],
        compiler_params=pltpu.CompilerParams(
            collective_id=0, has_side_effects=True, vmem_limit_bytes=56 * 1024 * 1024
        ),
        cost_estimate=pl.CostEstimate(
            flops=8 * shard_rows * width * units,
            bytes_accessed=4 * width * units,
            transcendentals=2 * shard_rows * units,
        ),
    )(tokens, cotangent, up_weight, down_weight)
    return pl.pallas_call(
        result_kernel,
        out_shape=(
            jax.ShapeDtypeStruct(tokens.shape, BF16),
            jax.ShapeDtypeStruct(tokens.shape, BF16),
            jax.ShapeDtypeStruct((feats, units), BF16),
            jax.ShapeDtypeStruct((units, feats), BF16),
        ),
        in_specs=[in_vmem] * 7,
        out_specs=[in_vmem] * 2 + [anywhere] * 2,
        scratch_shapes=[
            pltpu.VMEM((feats, units), BF16),
            pltpu.SemaphoreType.DMA((4,)),
            pltpu.SemaphoreType.DMA((8,)),
        ],
        compiler_params=pltpu.CompilerParams(vmem_limit_bytes=24 * 1024 * 1024),
        cost_estimate=pl.CostEstimate(
            flops=2 * n_dp * shard_rows * units * feats,
            bytes_accessed=4 * feats * units,
            transcendentals=0,
        ),
    )(tokens, cotangent, *exchanged)


def solution(mesh):
    return jax.shard_map(
        functools.partial(body, mesh.shape["dp"], mesh.shape["mp"]),
        mesh=mesh,
        in_specs=(P(("dp", "mp"), None), P(("dp", "mp"), None), P(None, "mp"), P("mp", None)),
        out_specs=(P(("dp", "mp"), None), P(("dp", "mp"), None), P("dp", "mp"), P("mp", "dp")),
        check_vma=False,
    )
```

```python
import functools

import jax
import jax.numpy as jnp
from jax import lax
from jax.experimental import pallas as pl
from jax.experimental.pallas import tpu as pltpu
from jax.sharding import PartitionSpec as P

ROOT_HALF = 0.7071067811865476
DENSITY_SCALE = 0.3989422804014327
TILE_ROWS = 16
HALVES = 2
MESH = pl.DeviceIdType.MESH
F32 = jnp.float32
BF16 = jnp.bfloat16


def chunk_of(size, choices=(512, 384, 256)):
    for choice in choices:
        if size % choice == 0:
            return choice
    return size


def dot(left, right, left_dim=1, right_dim=0):
    return lax.dot_general(
        left, right, (((left_dim,), (right_dim,)), ((), ())), preferred_element_type=F32
    )


def one_hot(wanted):
    return jnp.where(wanted, 1.0, 0.0).astype(BF16)


def relay_group(axis, n, send_sem, recv_sem, sent):
    other_axis = "mp" if axis == "dp" else "dp"
    me, fixed = lax.axis_index(axis), lax.axis_index(other_axis)
    lines = n // 2
    line, side = me // 2, me % 2

    def peer(block):
        to_line = lax.rem(line + block // 2, lines)
        to_side = side if block % 2 == 0 else 1 - side
        return {axis: 2 * to_line + to_side, other_axis: fixed}

    def start(kind, src, dst, block, to=None):
        copy = pltpu.make_async_remote_copy(
            src_ref=src, dst_ref=dst,
            send_sem=send_sem.at[kind, block], recv_sem=recv_sem.at[kind, block],
            device_id=peer(block if to is None else to), device_id_type=MESH,
        )
        copy.start()
        sent.append(copy)
        return copy

    def spread(kind, src, slots):
        straight = [start(kind, src, slots.at[2 * k], 2 * k) for k in range(1, lines)]
        return straight, [start(kind, src, slots.at[1], 1)]

    def pass_on(kind, slots, straight, crossed):
        for k in range(1, lines):
            straight[k - 1].wait_recv()
            crossed.append(start(kind, slots.at[2 * k], slots.at[2 * k + 1], 2 * k + 1, to=1))

    def opposite(block):
        return 2 * ((lines - block // 2) % lines) + block % 2

    return peer, start, spread, pass_on, opposite


def row_norm(tokens):
    centred = tokens - jnp.mean(tokens, axis=1, keepdims=True)
    variance = jnp.mean(centred * centred, axis=1, keepdims=True)
    inverse = lax.rsqrt(variance + 1e-06)
    return centred * inverse, inverse


def weight_grad(left, right, out, after=None):
    n_dp, shard_rows, lefts = left.shape
    step = chunk_of(lefts)
    right_rows = right[...].reshape(n_dp * shard_rows, right.shape[2])
    for i in range(lefts // step):
        cols = slice(i * step, (i + 1) * step)
        left_rows = left[:, :, cols].reshape(n_dp * shard_rows, step)
        out[cols, :] = dot(left_rows, right_rows, 0, 0).astype(BF16)
        if after is not None:
            after(i, cols)


def exchange_kernel(
    n_dp, n_mp,
    tokens_ref, cot_ref, up_hbm, down_hbm,
    rs_out, rs_grad, ncol, act, down_out,
    up_v, down_v,
    gather_n, gather_c, rs_out_send, rs_grad_send,
    ncol_send, ccol_send, ccol, hid, hid_own, act_own, slope, rows_n, rows_c,
    load_sem, own_sem, mp_send, mp_recv, dp_send, dp_recv,
):
    rows, width = tokens_ref.shape
    pieces = TILE_ROWS // rows
    wide = width // pieces
    shard_rows = rows * n_mp
    packed_rows = TILE_ROWS * n_mp
    units = up_v.shape[1]
    feats = width // n_dp

    loads = []
    parts = load_sem.shape[1]
    for w, (src, dst) in enumerate(((up_hbm, up_v), (down_hbm, down_v))):
        step = src.shape[0] // parts
        for i in range(parts):
            where = pl.ds(i * step, step)
            copy = pltpu.make_async_copy(src.at[where], dst.at[where], load_sem.at[w, i])
            copy.start()
            loads.append(copy)

    sent = []
    mp_peer, mp_start, mp_spread, mp_pass_on, mp_opposite = relay_group(
        "mp", n_mp, mp_send, mp_recv, sent
    )
    dp_peer, dp_start, dp_spread, dp_pass_on, dp_opposite = relay_group(
        "dp", n_dp, dp_send, dp_recv, sent
    )
    barrier = pltpu.get_barrier_semaphore()
    for b in range(1, n_mp):
        pl.semaphore_signal(barrier, inc=1, device_id=mp_peer(b), device_id_type=MESH)
    for b in range(1, n_dp):
        pl.semaphore_signal(barrier, inc=1, device_id=dp_peer(b), device_id_type=MESH)

    def pack(values):
        return jnp.concatenate(
            [values[:, q * wide:(q + 1) * wide] for q in range(pieces)], axis=0
        ).astype(BF16)

    xhat, _ = row_norm(tokens_ref[...].astype(F32))
    gather_n[0] = pack(xhat)
    gather_c[0] = pack(cot_ref[...].astype(F32))

    pl.semaphore_wait(barrier, n_mp - 1 + n_dp - 1)
    straight_n, crossed_n = mp_spread(0, gather_n.at[0], gather_n)
    straight_c, crossed_c = mp_spread(1, gather_c.at[0], gather_c)

    def home(packed):
        return packed % TILE_ROWS // rows * shard_rows + packed // TILE_ROWS * rows + packed % rows

    square = (packed_rows, packed_rows)
    first = lax.broadcasted_iota(jnp.int32, square, 0)
    second = lax.broadcasted_iota(jnp.int32, square, 1)
    packer = one_hot(second == home(first))
    unpacker = one_hot(first == home(second))

    def unpack(gathered, out):
        flat = dot(unpacker, gathered[...].reshape(packed_rows, wide)).astype(BF16)
        for q in range(pieces):
            out[:, q * wide:(q + 1) * wide] = flat[q * shard_rows:(q + 1) * shard_rows]

    own = []

    def keep(src, slots, which):
        copy = pltpu.make_async_copy(src, slots.at[0], own_sem.at[which])
        copy.start()
        own.append(copy)

    def send_columns(kind, out, blocks, slots):
        for j in range(n_dp):
            blocks[j] = out[:, j * feats:(j + 1) * feats]
        got = [
            dp_start(kind, blocks.at[dp_peer(b)["dp"]], slots.at[b], b) for b in range(1, n_dp)
        ]
        keep(blocks.at[lax.axis_index("dp")], slots, kind)
        return got

    mp_pass_on(0, gather_n, straight_n, crossed_n)
    mp_pass_on(1, gather_c, straight_c, crossed_c)
    for copy in crossed_n:
        copy.wait_recv()
    unpack(gather_n, rows_n)
    got_ncol = send_columns(0, rows_n, ncol_send, ncol)

    for copy in loads[:parts]:
        copy.wait()
    step = chunk_of(units)
    for i in range(units // step):
        cols = slice(i * step, (i + 1) * step)
        pre_act = dot(rows_n[...], up_v[:, cols])
        cumulative = 0.5 * (1.0 + lax.erf(pre_act * ROOT_HALF))
        density = jnp.exp(-0.5 * pre_act * pre_act) * DENSITY_SCALE
        hid_own[:, cols] = (pre_act * cumulative).astype(BF16)
        slope[:, cols] = cumulative + pre_act * density
    straight_h, crossed_h = dp_spread(2, hid_own, hid)
    keep(hid_own, hid, 2)

    for copy in crossed_c:
        copy.wait_recv()
    unpack(gather_c, rows_c)
    got_ccol = send_columns(1, rows_c, ccol_send, ccol)

    for copy in loads[parts:]:
        copy.wait()

    half = wide // HALVES

    def scatter(kind, partial_of, send, slots):
        got = []
        for h in range(HALVES):
            partial = partial_of(slice(h * pieces * half, (h + 1) * pieces * half)).astype(BF16)
            stacked = jnp.concatenate(
                [partial[:, q * half:(q + 1) * half] for q in range(pieces)], axis=0
            )
            total = dot(packer, stacked)
            send[h] = total.astype(BF16).reshape(n_mp, TILE_ROWS, half)
            got += [
                mp_start(kind + h, send.at[h, mp_opposite(b)], slots.at[h, b], b)
                for b in range(1, n_mp)
            ]
            keep(send.at[h, 0], slots.at[h], 2 + kind + h)
        return got

    got_out = scatter(2, lambda cols: dot(hid_own[...], down_v[:, cols]), rs_out_send, rs_out)
    for i in range(units // step):
        cols = slice(i * step, (i + 1) * step)
        hidden_grad = dot(rows_c[...], down_v[cols, :], 1, 1)
        act_own[:, cols] = (hidden_grad * slope[:, cols]).astype(BF16)
    straight_a, crossed_a = dp_spread(3, act_own, act)
    keep(act_own, act, 3)
    got_grad = scatter(
        2 + HALVES, lambda cols: dot(act_own[...], up_v[cols, :], 1, 1), rs_grad_send, rs_grad
    )
    dp_pass_on(2, hid, straight_h, crossed_h)
    dp_pass_on(3, act, straight_a, crossed_a)
    for copy in got_ccol + crossed_h:
        copy.wait_recv()
    for copy in own:
        copy.wait()
    weight_grad(hid, ccol, down_out)
    for copy in got_ncol + crossed_a:
        copy.wait_recv()
    for copy in got_grad + got_out:
        copy.wait_recv()
    for copy in sent:
        copy.wait_send()


def result_kernel(
    tokens_ref, cot_ref, rs_out, rs_grad, ncol, act, down_out,
    mixed_ref, tgrad_ref, up_grad_hbm, down_grad_hbm,
    up_out, down_sem, up_sem,
):
    rows, width = tokens_ref.shape
    pieces = TILE_ROWS // rows
    _, n_mp, _, half = rs_out.shape
    packed_rows = TILE_ROWS * n_mp
    stores = []

    def store(out, out_hbm, cols, sem):
        copy = pltpu.make_async_copy(out.at[cols], out_hbm.at[cols], sem)
        copy.start()
        stores.append(copy)

    parts = down_sem.shape[0]
    step = down_out.shape[0] // parts
    for i in range(parts):
        store(down_out, down_grad_hbm, slice(i * step, (i + 1) * step), down_sem.at[i])
    weight_grad(ncol, act, up_out, lambda i, cols: store(up_out, up_grad_hbm, cols, up_sem.at[i]))

    at = lax.broadcasted_iota(jnp.int32, (8, packed_rows), 0)
    to = lax.broadcasted_iota(jnp.int32, (8, packed_rows), 1) % TILE_ROWS
    adders = [one_hot((to == at + q * rows) & (at < rows)) for q in range(pieces)]

    def summed(slots):
        flats = [slots[h].reshape(packed_rows, half) for h in range(HALVES)]
        return jnp.concatenate(
            [dot(adders[q], flat)[:rows] for flat in flats for q in range(pieces)], axis=1
        )

    tokens = tokens_ref[...].astype(F32)
    xhat, inverse = row_norm(tokens)
    mixed_ref[...] = (tokens + summed(rs_out)).astype(BF16)
    grad = summed(rs_grad)
    grad_mean = jnp.mean(grad, axis=1, keepdims=True)
    projection = jnp.mean(grad * xhat, axis=1, keepdims=True)
    tgrad_ref[...] = (
        cot_ref[...].astype(F32) + inverse * (grad - grad_mean - xhat * projection)
    ).astype(BF16)
    for copy in stores:
        copy.wait()


def body(n_dp, n_mp, tokens, cotangent, up_weight, down_weight):
    rows, width = tokens.shape
    units = up_weight.shape[1]
    feats = width // n_dp
    shard_rows = rows * n_mp
    wide = width * rows // TILE_ROWS
    packed = (n_mp, TILE_ROWS, wide)
    scattered = (HALVES, n_mp, TILE_ROWS, wide // HALVES)
    columns = (n_dp, shard_rows, feats)
    hiddens = (n_dp, shard_rows, units)
    in_vmem, anywhere = pl.BlockSpec(memory_space=pltpu.VMEM), pl.BlockSpec(memory_space=pl.ANY)
    exchanged = pl.pallas_call(
        functools.partial(exchange_kernel, n_dp, n_mp),
        out_shape=[
            pltpu.VMEM(shape, BF16)
            for shape in (scattered, scattered, columns, hiddens, (units, feats))
        ],
        in_specs=[in_vmem] * 2 + [anywhere] * 2,
        out_specs=[in_vmem] * 5,
        scratch_shapes=[
            pltpu.VMEM(up_weight.shape, BF16),
            pltpu.VMEM(down_weight.shape, BF16),
            *[pltpu.VMEM(packed, BF16)] * 2,
            *[pltpu.VMEM(scattered, BF16)] * 2,
            *[pltpu.VMEM(columns, BF16)] * 3,
            pltpu.VMEM(hiddens, BF16),
            *[pltpu.VMEM(hiddens[1:], BF16)] * 2,
            pltpu.VMEM((shard_rows, units), F32),
            *[pltpu.VMEM((shard_rows, width), BF16)] * 2,
            pltpu.SemaphoreType.DMA((2, 4)),
            pltpu.SemaphoreType.DMA((4 + 2 * HALVES,)),
            pltpu.SemaphoreType.DMA((2 + 2 * HALVES, n_mp)),
            pltpu.SemaphoreType.DMA((2 + 2 * HALVES, n_mp)),
            pltpu.SemaphoreType.DMA((4, n_dp)),
            pltpu.SemaphoreType.DMA((4, n_dp)),
        ],
        compiler_params=pltpu.CompilerParams(
            collective_id=0, has_side_effects=True, vmem_limit_bytes=56 * 1024 * 1024
        ),
        cost_estimate=pl.CostEstimate(
            flops=8 * shard_rows * width * units,
            bytes_accessed=4 * width * units,
            transcendentals=2 * shard_rows * units,
        ),
    )(tokens, cotangent, up_weight, down_weight)
    return pl.pallas_call(
        result_kernel,
        out_shape=(
            jax.ShapeDtypeStruct(tokens.shape, BF16),
            jax.ShapeDtypeStruct(tokens.shape, BF16),
            jax.ShapeDtypeStruct((feats, units), BF16),
            jax.ShapeDtypeStruct((units, feats), BF16),
        ),
        in_specs=[in_vmem] * 7,
        out_specs=[in_vmem] * 2 + [anywhere] * 2,
        scratch_shapes=[
            pltpu.VMEM((feats, units), BF16),
            pltpu.SemaphoreType.DMA((4,)),
            pltpu.SemaphoreType.DMA((8,)),
        ],
        compiler_params=pltpu.CompilerParams(vmem_limit_bytes=24 * 1024 * 1024),
        cost_estimate=pl.CostEstimate(
            flops=2 * n_dp * shard_rows * units * feats,
            bytes_accessed=4 * feats * units,
            transcendentals=0,
        ),
    )(tokens, cotangent, *exchanged)


def solution(mesh):
    return jax.shard_map(
        functools.partial(body, mesh.shape["dp"], mesh.shape["mp"]),
        mesh=mesh,
        in_specs=(P(("dp", "mp"), None), P(("dp", "mp"), None), P(None, "mp"), P("mp", None)),
        out_specs=(P(("dp", "mp"), None), P(("dp", "mp"), None), P("dp", "mp"), P("mp", "dp")),
        check_vma=False,
    )
```
